512 devices in a mesh: gx: 32 (over z_lo, y), gy: 16 (over z_hi, x, core).
Axes of the slice: x: 4, y: 8, z: 8 (z_hi: 2, z_lo: 4; z = z_hi * 4 + z_lo), core: 2. Of those that a mesh axis runs over, the one named last changes fastest.
Arguments:
- start_state: float32 [5, 256, 256, 256], P(None, 'gx', 'gy'), may hold values from -1.5 to 5.5, as said below
- section_state: float32 [5, 256, 256, 256], P(None, 'gx', 'gy'), may hold values from -1.5 to 5.5, as said below
- previous_speed: float32 [], replicated, may hold values from 1.2 to 2.4
Outputs:
- new_state: float32 [5, 256, 256, 256], P(None, 'gx', 'gy')
- next_speed: float32 [], replicated
The draws below stay inside these ranges and needn't reach their ends.
Inputs may be any that keep to these rules, and one draw needn't show every extreme that they name: `start_state`: density (component 0) lies in 0.7 to 1.3 and the pressure 0.4 (E - |momentum|^2 / (2 density)) in 0.6 to 1.2 in every cell. `section_state`: density (component 0) lies in 0.7 to 1.3 and the pressure 0.4 (E - |momentum|^2 / (2 density)) in 0.6 to 1.2 in every cell.
All inputs are finite; a program needn't handle non-finite values.
Results may differ from the reference program's by a relative error of at most 0.00002.
Values sent between devices are 32-bit elements; how exact they have to be, the bound alone decides.
No kernel may reach another device: no remote copies, remote signals or barrier semaphores. Data moves between devices by JAX's collectives and lax.ppermute only.
A program may use at most 64 MiB of HBM per device.

```python
import math
import jax
import jax.numpy as jnp

CX = 8
CY = 16
NZ = 256
NX = 256
NY = 256


GAMMA = 1.4


def periodic_offset(count, centre):
    offset = (jnp.arange(count, dtype=jnp.int32) - centre + count // 2) % count - count // 2
    return offset.astype(jnp.float32)


def bump_field(base_key):
    subkeys = jax.random.split(jax.random.fold_in(base_key, 5), 3)
    centre_x = jax.random.randint(subkeys[0], (), 0, NX, dtype=jnp.int32)
    centre_y = jax.random.randint(subkeys[1], (), 0, NY, dtype=jnp.int32)
    centre_z = jax.random.randint(subkeys[2], (), 0, NZ, dtype=jnp.int32)
    wide_x = float(max(NX // 32, 2))
    wide_y = float(max(NY // 32, 2))
    wide_z = float(max(NZ // 16, 2))
    along_x = (periodic_offset(NX, centre_x) / wide_x) ** 2
    along_y = (periodic_offset(NY, centre_y) / wide_y) ** 2
    along_z = (periodic_offset(NZ, centre_z) / wide_z) ** 2
    exponent = along_x[:, None, None] + along_y[None, :, None] + along_z[None, None, :]
    return jnp.exp(-0.5 * exponent)


def make_state(key, base_key):
    subkeys = jax.random.split(key, 3)
    amplitude = (0.2 + 0.25 * bump_field(base_key))[None]
    jitter = jnp.clip(jax.random.normal(subkeys[0], (3, NX, NY, NZ), jnp.float32), -2.5, 2.5)
    flow_speed_vector = amplitude * jitter
    density = 1.0 + 0.3 * jax.random.uniform(subkeys[1], (NX, NY, NZ), jnp.float32, -1.0, 1.0)
    thermodynamic_load = 0.9 + 0.3 * jax.random.uniform(subkeys[2], (NX, NY, NZ), jnp.float32, -1.0, 1.0)
    energy = thermodynamic_load / (GAMMA - 1.0) + 0.5 * density * jnp.sum(flow_speed_vector * flow_speed_vector, axis=0)
    return jnp.concatenate([density[None], density[None] * flow_speed_vector, energy[None]], axis=0)


def draw_start_state(key, part):
    return make_state(jax.random.fold_in(key, 11), key)


def draw_section_state(key, part):
    return make_state(jax.random.fold_in(key, 23), key)


def setup_inputs(seed: int = 0) -> dict:
    key_list = jax.random.split(jax.random.key(seed), 4)
    start_state = draw_start_state(jax.random.fold_in(key_list[3], 71), 0)
    section_state = draw_section_state(jax.random.fold_in(key_list[3], 71), 0)
    previous_speed = jnp.clip(jnp.exp(jax.random.uniform(key_list[2], (), jnp.float32, math.log(1.2), math.log(2.4))), 1.2, 2.4)
    return {"start_state": start_state, "section_state": section_state, "previous_speed": previous_speed}


GAMMA = 1.4
COURANT = 0.3
VISCOSITY = 0.05
CONDUCTION = 0.07
FIRST = (0.8, -0.2, 4.0 / 105.0, -1.0 / 280.0)
SECOND = (1.6, -0.2, 8.0 / 315.0, -1.0 / 560.0)
CENTRE = -205.0 / 72.0

def primitive(conserved_variables):
    density = conserved_variables[0]
    flow_speed_vector = (conserved_variables[1] / density, conserved_variables[2] / density, conserved_variables[3] / density)
    kinetic = 0.5 * (flow_speed_vector[0] * flow_speed_vector[0] + flow_speed_vector[1] * flow_speed_vector[1] + flow_speed_vector[2] * flow_speed_vector[2])
    thermodynamic_load = (GAMMA - 1.0) * (conserved_variables[4] - density * kinetic)
    return (density, flow_speed_vector, kinetic, thermodynamic_load)

def wave_speed(conserved_variables):
    density, flow_speed_vector, kinetic, thermodynamic_load = primitive(conserved_variables)
    return jnp.sqrt(2.0 * kinetic) + jnp.sqrt(GAMMA * thermodynamic_load / density)

def quantities(conserved_variables, sweep_coordinate):
    density, flow_speed_vector, kinetic, thermodynamic_load = primitive(conserved_variables)
    transported_scalar = flow_speed_vector[sweep_coordinate]
    interface_transport = [conserved_variables[0] * transported_scalar]
    for variable_index in range(3):
        tendency_increment = conserved_variables[1 + variable_index] * transported_scalar
        if variable_index == sweep_coordinate:
            tendency_increment = tendency_increment + thermodynamic_load
        interface_transport.append(tendency_increment)
    interface_transport.append((conserved_variables[4] + thermodynamic_load) * transported_scalar)
    return interface_transport + [flow_speed_vector[0], flow_speed_vector[1], flow_speed_vector[2], kinetic, thermodynamic_load / density]

def derivatives(section_terms, start_terms, along_axis, block, extent):
    position = jnp.arange(extent)
    home_block = position // block
    shape = [1, 1, 1]
    shape[along_axis] = extent
    inside = {}
    for offset in (1, 2, 3, 4, -1, -2, -3, -4):
        inside[offset] = ((position + offset) % extent // block == home_block).reshape(shape)

    def neighbour(variable_index, offset):
        current = jnp.roll(section_terms[variable_index], -offset, along_axis)
        if start_terms is None:
            return current
        earlier = jnp.roll(start_terms[variable_index], -offset, along_axis)
        return jnp.where(inside[offset], current, earlier)
    firsts = []
    seconds = []
    for variable_index in range(10):
        if variable_index < 5:
            result = jnp.zeros_like(section_terms[variable_index])
            for offset in range(4):
                result = result + FIRST[offset] * (neighbour(variable_index, offset + 1) - neighbour(variable_index, -offset - 1))
            firsts.append(result)
        else:
            result = CENTRE * section_terms[variable_index]
            for offset in range(4):
                result = result + SECOND[offset] * (neighbour(variable_index, offset + 1) + neighbour(variable_index, -offset - 1))
            seconds.append(result)
    return (firsts, seconds)

def assemble(parts):
    rate = []
    for variable_index in range(5):
        rate.append(-(parts[0][0][variable_index] + parts[1][0][variable_index] + parts[2][0][variable_index]))
    lap = [parts[0][1][variable_index] + parts[1][1][variable_index] + parts[2][1][variable_index] for variable_index in range(5)]
    rate[1] = rate[1] + VISCOSITY * lap[0]
    rate[2] = rate[2] + VISCOSITY * lap[1]
    rate[3] = rate[3] + VISCOSITY * lap[2]
    rate[4] = rate[4] + VISCOSITY * lap[3] + CONDUCTION * lap[4]
    return jnp.stack(rate, 0)

def reference(start_state, section_state, previous_speed):
    x_parts = derivatives(quantities(section_state, 0), quantities(start_state, 0), 0, CX, NX)
    y_parts = derivatives(quantities(section_state, 1), quantities(start_state, 1), 1, CY, NY)
    z_parts = derivatives(quantities(section_state, 2), None, 2, NZ, NZ)
    rate = assemble((x_parts, y_parts, z_parts))
    time_step = COURANT / previous_speed
    new_state = 0.75 * start_state + 0.25 * (section_state + time_step * rate)
    next_speed = jnp.max(wave_speed(new_state))
    return (new_state, next_speed)
```

```python
import jax
import jax.numpy as jnp
from jax import lax
from jax.experimental import pallas as pl
from jax.experimental.pallas import tpu as pltpu
from jax.sharding import PartitionSpec as P

GAMMA = 1.4
COURANT = 0.3
VISCOSITY = 0.05
CONDUCTION = 0.07
FIRST = (0.8, -0.2, 4.0 / 105.0, -1.0 / 280.0)
SECOND = (1.6, -0.2, 8.0 / 315.0, -1.0 / 560.0)
CENTRE = -205.0 / 72.0
VMEM = pltpu.VMEM
SMEM = pltpu.SMEM


def primitive(q):
    inverse = 1.0 / q[0]
    u, v, w = q[1] * inverse, q[2] * inverse, q[3] * inverse
    kinetic = 0.5 * (u * u + v * v + w * w)
    pressure = (GAMMA - 1.0) * (q[4] - q[0] * kinetic)
    return inverse, (u, v, w), kinetic, pressure


def flux(q, velocity, pressure, d):
    s = velocity[d]
    out = [q[1 + d], q[1] * s, q[2] * s, q[3] * s, (q[4] + pressure) * s]
    out[1 + d] = out[1 + d] + pressure
    return out


def smooth(inverse, velocity, kinetic, pressure):
    heat = VISCOSITY * kinetic + CONDUCTION * (pressure * inverse)
    return [None] + [VISCOSITY * s for s in velocity] + [heat]


def sides(f, g, m):
    first = FIRST[m - 1] * f
    if g is None:
        return -first, first
    second = SECOND[m - 1] * g
    return second - first, second + first


def pack_kernel(start, x_low, x_high, y_low, y_high):
    x_low[...] = start[:, 0:4]
    x_high[...] = start[:, 4:8]
    first = lax.broadcasted_iota(jnp.int32, (8, 256), 0) < 4
    for c in range(5):
        for j in range(4):
            even, odd = start[c, 2 * j, 0:8], start[c, 2 * j + 1, 0:8]
            y_low[c, j] = jnp.where(first, even, pltpu.roll(odd, 4, 0))
            even, odd = start[c, 2 * j, 8:16], start[c, 2 * j + 1, 8:16]
            y_high[c, j] = jnp.where(first, pltpu.roll(odd, 4, 0), even)


def inner_kernel(speed, start, section, out, fluxes, smooths):
    rows = lax.broadcasted_iota(jnp.int32, (16, 256), 0)

    def layer(i, carry):
        q = [section[c, i] for c in range(5)]
        inverse, velocity, kinetic, pressure = primitive(q)
        g = smooth(inverse, velocity, kinetic, pressure)
        fx = flux(q, velocity, pressure, 0)
        fy = flux(q, velocity, pressure, 1)
        fz = flux(q, velocity, pressure, 2)
        for c in range(5):
            fluxes[c, i] = fx[c]
            total = jnp.zeros((16, 256), jnp.float32)
            if c:
                smooths[c - 1, i] = g[c]
                total = (3.0 * CENTRE) * g[c]
            for m in range(1, 5):
                up, down = sides(fz[c], g[c], m)
                total = total + pltpu.roll(up, 256 - m, 1) + pltpu.roll(down, m, 1)
                up, down = sides(fy[c], g[c], m)
                total = total + jnp.where(rows < 16 - m, pltpu.roll(up, 16 - m, 0), 0.0)
                total = total + jnp.where(rows >= m, pltpu.roll(down, m, 0), 0.0)
            out[c, i] = total
        return carry

    lax.fori_loop(0, 8, layer, 0)
    factor = (0.25 * COURANT) / jnp.full((16, 256), speed[0], jnp.float32)
    for c in range(5):
        for i in range(8):
            total = out[c, i]
            for m in range(1, 5):
                for j, sign in ((i + m, -1.0), (i - m, 1.0)):
                    if 0 <= j < 8:
                        total = total + (sign * FIRST[m - 1]) * fluxes[c, j]
                        if c:
                            total = total + SECOND[m - 1] * smooths[c - 1, j]
            out[c, i] = 0.75 * start[c, i] + 0.25 * section[c, i] + factor * total


def rim_kernel(speed, inner, x_low, x_high, y_low, y_high, out, peak, fluxes, smooths, sums):
    rows = lax.broadcasted_iota(jnp.int32, (8, 256), 0)
    first = rows < 4

    def x_rim(i, carry):
        for k, side in enumerate((x_low, x_high)):
            q = [side[c, i] for c in range(5)]
            inverse, velocity, kinetic, pressure = primitive(q)
            g = smooth(inverse, velocity, kinetic, pressure)
            f = flux(q, velocity, pressure, 0)
            for c in range(5):
                fluxes[k, c, i] = f[c]
                if c:
                    smooths[k, c - 1, i] = g[c]
        return carry

    def y_rim(j, carry):
        for odd in range(2):
            q = []
            for c in range(5):
                low, high = y_low[c, j], y_high[c, j]
                q.append(jnp.where(first, low, high) if odd else jnp.where(first, high, low))
            inverse, velocity, kinetic, pressure = primitive(q)
            g = smooth(inverse, velocity, kinetic, pressure)
            f = flux(q, velocity, pressure, 1)
            turn = 4 * odd
            for c in range(5):
                lower = jnp.zeros((8, 256), jnp.float32)
                upper = jnp.zeros((8, 256), jnp.float32)
                for m in range(1, 5):
                    up, down = sides(f[c], g[c], m)
                    lower = lower + jnp.where(rows < m, pltpu.roll(down, (m + turn) % 8, 0), 0.0)
                    upper = upper + jnp.where(rows >= 8 - m, pltpu.roll(up, (8 - m + turn) % 8, 0), 0.0)
                sums[c, 2 * j + odd, 0:8] = lower
                sums[c, 2 * j + odd, 8:16] = upper
        return carry

    lax.fori_loop(0, 4, x_rim, 0)
    lax.fori_loop(0, 4, y_rim, 0)
    factor = (0.25 * COURANT) / jnp.full((16, 256), speed[0], jnp.float32)
    most = jnp.zeros((16, 256), jnp.float32)
    for i in range(8):
        new = []
        for c in range(5):
            total = sums[c, i]
            for m in range(1, 5):
                for k, j, sign in ((0, i - m, 1.0), (1, i + m - 8, -1.0)):
                    j = j + 4 if k == 0 else j
                    if (k == 0 and i - m < 0) or (k == 1 and i + m > 7):
                        total = total + (sign * FIRST[m - 1]) * fluxes[k, c, j]
                        if c:
                            total = total + SECOND[m - 1] * smooths[k, c - 1, j]
            value = inner[c, i] + factor * total
            out[c, i] = value
            new.append(value)
        inverse, velocity, kinetic, pressure = primitive(new)
        most = jnp.maximum(most, jnp.sqrt(2.0 * kinetic) + jnp.sqrt(GAMMA * pressure * inverse))
    peak[...] = jnp.full(peak.shape, jnp.max(most), jnp.float32)


def shape(*sizes):
    return jax.ShapeDtypeStruct(sizes, jnp.float32)


def in_vmem(n):
    return [pl.BlockSpec(memory_space=VMEM)] * n


def call(kernel, outs, n_in, scratch, speed, *arrays):
    specs = in_vmem(n_in)
    if speed is not None:
        specs = [pl.BlockSpec(memory_space=SMEM)] + specs
        arrays = (speed,) + arrays
    return pl.pallas_call(
        kernel,
        out_shape=outs,
        in_specs=specs,
        out_specs=tuple(in_vmem(len(outs))),
        scratch_shapes=scratch,
        compiler_params=pltpu.CompilerParams(vmem_limit_bytes=24 << 20),
    )(*arrays)


def shift(x, axis, by):
    n = lax.axis_size(axis)
    return lax.ppermute(x, axis, [(i, (i + by) % n) for i in range(n)])


def local(start, section, previous_speed):
    speed = previous_speed.reshape(1)
    devices = lax.axis_size(("gx", "gy"))
    x_low, x_high, y_low, y_high = call(
        pack_kernel,
        (shape(5, 4, 16, 256), shape(5, 4, 16, 256), shape(5, 4, 8, 256), shape(5, 4, 8, 256)),
        1,
        [],
        None,
        start,
    )
    from_high_x, from_low_x = shift(x_low, "gx", -1), shift(x_high, "gx", 1)
    from_high_y, from_low_y = shift(y_low, "gy", -1), shift(y_high, "gy", 1)
    (inner,) = call(
        inner_kernel,
        (shape(5, 8, 16, 256),),
        2,
        [VMEM((5, 8, 16, 256), jnp.float32), VMEM((4, 8, 16, 256), jnp.float32)],
        speed,
        start,
        section,
    )
    new, peak = call(
        rim_kernel,
        (shape(5, 8, 16, 256), shape(devices, 128)),
        5,
        [
            VMEM((2, 5, 4, 16, 256), jnp.float32),
            VMEM((2, 4, 4, 16, 256), jnp.float32),
            VMEM((5, 8, 16, 256), jnp.float32),
        ],
        speed,
        inner,
        from_low_x,
        from_high_x,
        from_low_y,
        from_high_y,
    )
    peaks = lax.all_to_all(peak, ("gx", "gy"), 0, 0, tiled=True)
    return new, jnp.max(peaks)


def solution(mesh):
    spec = P(None, "gx", "gy", None)
    return jax.shard_map(
        local, mesh=mesh, in_specs=(spec, spec, P()), out_specs=(spec, P()), check_vma=False
    )
```

```python
import jax
import jax.numpy as jnp
from jax import lax
from jax.experimental import pallas as pl
from jax.experimental.pallas import tpu as pltpu
from jax.sharding import PartitionSpec as P

GAMMA = 1.4
COURANT = 0.3
VISCOSITY = 0.05
CONDUCTION = 0.07
FIRST = (0.8, -0.2, 4.0 / 105.0, -1.0 / 280.0)
SECOND = (1.6, -0.2, 8.0 / 315.0, -1.0 / 560.0)
CENTRE = -205.0 / 72.0
VMEM = pltpu.VMEM
SMEM = pltpu.SMEM


def primitive(q):
    inverse = 1.0 / q[0]
    u, v, w = q[1] * inverse, q[2] * inverse, q[3] * inverse
    kinetic = 0.5 * (u * u + v * v + w * w)
    pressure = (GAMMA - 1.0) * (q[4] - q[0] * kinetic)
    return inverse, (u, v, w), kinetic, pressure


def flux(q, velocity, pressure, d):
    s = velocity[d]
    out = [q[1 + d], q[1] * s, q[2] * s, q[3] * s, (q[4] + pressure) * s]
    out[1 + d] = out[1 + d] + pressure
    return out


def smooth(inverse, velocity, kinetic, pressure):
    heat = VISCOSITY * kinetic + CONDUCTION * (pressure * inverse)
    return [None] + [VISCOSITY * s for s in velocity] + [heat]


def sides(f, g, m):
    first = FIRST[m - 1] * f
    if g is None:
        return -first, first
    second = SECOND[m - 1] * g
    return second - first, second + first


def odd(axis):
    return lax.rem(lax.axis_index(axis), 2)


def pack_kernel(start, x_even, x_odd, y_even, y_odd):
    side = odd("gx")
    x_even[...] = start[:, pl.ds(4 - 4 * side, 4)]
    x_odd[...] = start[:, pl.ds(4 * side, 4)]
    first = lax.broadcasted_iota(jnp.int32, (8, 256), 0) < 4
    upper = odd("gy") == 0
    for c in range(5):
        for j in range(4):
            a, b = start[c, 2 * j, 0:8], start[c, 2 * j + 1, 0:8]
            low = jnp.where(first, a, pltpu.roll(b, 4, 0))
            a, b = start[c, 2 * j, 8:16], start[c, 2 * j + 1, 8:16]
            high = jnp.where(first, pltpu.roll(b, 4, 0), a)
            y_even[c, j] = jnp.where(upper, high, low)
            y_odd[c, j] = jnp.where(upper, low, high)


def inner_kernel(speed, start, section, out, fluxes, smooths):
    rows = lax.broadcasted_iota(jnp.int32, (16, 256), 0)

    def layer(i, carry):
        q = [section[c, i] for c in range(5)]
        inverse, velocity, kinetic, pressure = primitive(q)
        g = smooth(inverse, velocity, kinetic, pressure)
        fx = flux(q, velocity, pressure, 0)
        fy = flux(q, velocity, pressure, 1)
        fz = flux(q, velocity, pressure, 2)
        for c in range(5):
            fluxes[c, i] = fx[c]
            total = jnp.zeros((16, 256), jnp.float32)
            if c:
                smooths[c - 1, i] = g[c]
                total = (3.0 * CENTRE) * g[c]
            for m in range(1, 5):
                up, down = sides(fz[c], g[c], m)
                total = total + pltpu.roll(up, 256 - m, 1) + pltpu.roll(down, m, 1)
                up, down = sides(fy[c], g[c], m)
                total = total + jnp.where(rows < 16 - m, pltpu.roll(up, 16 - m, 0), 0.0)
                total = total + jnp.where(rows >= m, pltpu.roll(down, m, 0), 0.0)
            out[c, i] = total
        return carry

    lax.fori_loop(0, 8, layer, 0)
    factor = (0.25 * COURANT) / jnp.full((16, 256), speed[0], jnp.float32)
    for c in range(5):
        for i in range(8):
            total = out[c, i]
            for m in range(1, 5):
                for j, sign in ((i + m, -1.0), (i - m, 1.0)):
                    if 0 <= j < 8:
                        total = total + (sign * FIRST[m - 1]) * fluxes[c, j]
                        if c:
                            total = total + SECOND[m - 1] * smooths[c - 1, j]
            out[c, i] = 0.75 * start[c, i] + 0.25 * section[c, i] + factor * total


def rim_kernel(speed, inner, x_even, x_odd, y_even, y_odd, out, peak, fluxes, smooths, sums):
    rows = lax.broadcasted_iota(jnp.int32, (8, 256), 0)
    even_first = (rows // 4) == odd("gy")
    below = odd("gx")

    def x_rim(i, carry):
        for k, side in ((1 - below, x_even), (below, x_odd)):
            q = [side[c, i] for c in range(5)]
            inverse, velocity, kinetic, pressure = primitive(q)
            g = smooth(inverse, velocity, kinetic, pressure)
            f = flux(q, velocity, pressure, 0)
            for c in range(5):
                fluxes[k, c, i] = f[c]
                if c:
                    smooths[k, c - 1, i] = g[c]
        return carry

    def y_rim(j, carry):
        for second in range(2):
            q = []
            for c in range(5):
                a, b = (y_odd, y_even) if second else (y_even, y_odd)
                q.append(jnp.where(even_first, a[c, j], b[c, j]))
            inverse, velocity, kinetic, pressure = primitive(q)
            g = smooth(inverse, velocity, kinetic, pressure)
            f = flux(q, velocity, pressure, 1)
            turn = 4 * second
            for c in range(5):
                lower = jnp.zeros((8, 256), jnp.float32)
                upper = jnp.zeros((8, 256), jnp.float32)
                for m in range(1, 5):
                    up, down = sides(f[c], g[c], m)
                    lower = lower + jnp.where(rows < m, pltpu.roll(down, (m + turn) % 8, 0), 0.0)
                    upper = upper + jnp.where(rows >= 8 - m, pltpu.roll(up, (8 - m + turn) % 8, 0), 0.0)
                sums[c, 2 * j + second, 0:8] = lower
                sums[c, 2 * j + second, 8:16] = upper
        return carry

    lax.fori_loop(0, 4, x_rim, 0)
    lax.fori_loop(0, 4, y_rim, 0)
    factor = (0.25 * COURANT) / jnp.full((16, 256), speed[0], jnp.float32)
    most = jnp.zeros((16, 256), jnp.float32)
    for i in range(8):
        new = []
        for c in range(5):
            total = sums[c, i]
            for m in range(1, 5):
                for k, j, sign in ((0, i - m, 1.0), (1, i + m - 8, -1.0)):
                    j = j + 4 if k == 0 else j
                    if (k == 0 and i - m < 0) or (k == 1 and i + m > 7):
                        total = total + (sign * FIRST[m - 1]) * fluxes[k, c, j]
                        if c:
                            total = total + SECOND[m - 1] * smooths[k, c - 1, j]
            value = inner[c, i] + factor * total
            out[c, i] = value
            new.append(value)
        inverse, velocity, kinetic, pressure = primitive(new)
        most = jnp.maximum(most, jnp.sqrt(2.0 * kinetic) + jnp.sqrt(GAMMA * pressure * inverse))
    peak[...] = jnp.full(peak.shape, jnp.max(most), jnp.float32)


def shape(*sizes):
    return jax.ShapeDtypeStruct(sizes, jnp.float32)


def in_vmem(n):
    return [pl.BlockSpec(memory_space=VMEM)] * n


def call(kernel, outs, n_in, scratch, speed, *arrays):
    specs = in_vmem(n_in)
    if speed is not None:
        specs = [pl.BlockSpec(memory_space=SMEM)] + specs
        arrays = (speed,) + arrays
    return pl.pallas_call(
        kernel,
        out_shape=outs,
        in_specs=specs,
        out_specs=tuple(in_vmem(len(outs))),
        scratch_shapes=scratch,
        compiler_params=pltpu.CompilerParams(vmem_limit_bytes=24 << 20),
    )(*arrays)


def swap(x, axis, offset):
    n = lax.axis_size(axis)
    pairs = [((i + offset) % n, (i + 1 + offset) % n) for i in range(0, n, 2)]
    return lax.ppermute(x, axis, pairs + [(b, a) for a, b in pairs])


def local(start, section, previous_speed):
    speed = previous_speed.reshape(1)
    devices = lax.axis_size(("gx", "gy"))
    x_even, x_odd, y_even, y_odd = call(
        pack_kernel,
        (shape(5, 4, 16, 256), shape(5, 4, 16, 256), shape(5, 4, 8, 256), shape(5, 4, 8, 256)),
        1,
        [],
        None,
        start,
    )
    received = (
        swap(x_even, "gx", 0),
        swap(x_odd, "gx", 1),
        swap(y_even, "gy", 0),
        swap(y_odd, "gy", 1),
    )
    (inner,) = call(
        inner_kernel,
        (shape(5, 8, 16, 256),),
        2,
        [VMEM((5, 8, 16, 256), jnp.float32), VMEM((4, 8, 16, 256), jnp.float32)],
        speed,
        start,
        section,
    )
    new, peak = call(
        rim_kernel,
        (shape(5, 8, 16, 256), shape(devices, 128)),
        5,
        [
            VMEM((2, 5, 4, 16, 256), jnp.float32),
            VMEM((2, 4, 4, 16, 256), jnp.float32),
            VMEM((5, 8, 16, 256), jnp.float32),
        ],
        speed,
        inner,
        *received,
    )
    peaks = lax.all_to_all(peak, ("gx", "gy"), 0, 0, tiled=True)
    return new, jnp.max(peaks)


def solution(mesh):
    spec = P(None, "gx", "gy", None)
    return jax.shard_map(
        local, mesh=mesh, in_specs=(spec, spec, P()), out_specs=(spec, P()), check_vma=False
    )
```

```python
import jax
import jax.numpy as jnp
from jax import lax
from jax.experimental import pallas as pl
from jax.experimental.pallas import tpu as pltpu
from jax.sharding import PartitionSpec as P

GAMMA = 1.4
COURANT = 0.3
VISCOSITY = 0.05
CONDUCTION = 0.07
FIRST = (0.8, -0.2, 4.0 / 105.0, -1.0 / 280.0)
SECOND = (1.6, -0.2, 8.0 / 315.0, -1.0 / 560.0)
CENTRE = -205.0 / 72.0
VMEM = pltpu.VMEM
SMEM = pltpu.SMEM


def primitive(q):
    inverse = 1.0 / q[0]
    u, v, w = q[1] * inverse, q[2] * inverse, q[3] * inverse
    kinetic = 0.5 * (u * u + v * v + w * w)
    pressure = (GAMMA - 1.0) * (q[4] - q[0] * kinetic)
    return inverse, (u, v, w), kinetic, pressure


def flux(q, velocity, pressure, d):
    s = velocity[d]
    out = [q[1 + d], q[1] * s, q[2] * s, q[3] * s, (q[4] + pressure) * s]
    out[1 + d] = out[1 + d] + pressure
    return out


def smooth(inverse, velocity, kinetic, pressure):
    heat = VISCOSITY * kinetic + CONDUCTION * (pressure * inverse)
    return [None] + [VISCOSITY * s for s in velocity] + [heat]


def sides(f, g, m):
    first = FIRST[m - 1] * f
    if g is None:
        return -first, first
    second = SECOND[m - 1] * g
    return second - first, second + first


def odd(axis):
    return lax.rem(lax.axis_index(axis), 2)


def pack_kernel(start, x_even, x_odd, y_even, y_odd):
    side = odd("gx")
    x_even[...] = start[:, pl.ds(4 - 4 * side, 4)]
    x_odd[...] = start[:, pl.ds(4 * side, 4)]
    first = lax.broadcasted_iota(jnp.int32, (8, 256), 0) < 4
    upper = odd("gy") == 0
    for c in range(5):
        for j in range(4):
            a, b = start[c, 2 * j, 0:8], start[c, 2 * j + 1, 0:8]
            low = jnp.where(first, a, pltpu.roll(b, 4, 0))
            a, b = start[c, 2 * j, 8:16], start[c, 2 * j + 1, 8:16]
            high = jnp.where(first, pltpu.roll(b, 4, 0), a)
            y_even[c, j] = jnp.where(upper, high, low)
            y_odd[c, j] = jnp.where(upper, low, high)


def inner_kernel(speed, start, section, out, fluxes, smooths):
    rows = lax.broadcasted_iota(jnp.int32, (16, 256), 0)

    def layer(i, carry):
        q = [section[c, i] for c in range(5)]
        inverse, velocity, kinetic, pressure = primitive(q)
        g = smooth(inverse, velocity, kinetic, pressure)
        fx = flux(q, velocity, pressure, 0)
        fy = flux(q, velocity, pressure, 1)
        fz = flux(q, velocity, pressure, 2)
        for c in range(5):
            fluxes[c, i] = fx[c]
            total = jnp.zeros((16, 256), jnp.float32)
            if c:
                smooths[c - 1, i] = g[c]
                total = (3.0 * CENTRE) * g[c]
            for m in range(1, 5):
                up, down = sides(fz[c], g[c], m)
                total = total + pltpu.roll(up, 256 - m, 1) + pltpu.roll(down, m, 1)
                up, down = sides(fy[c], g[c], m)
                total = total + jnp.where(rows < 16 - m, pltpu.roll(up, 16 - m, 0), 0.0)
                total = total + jnp.where(rows >= m, pltpu.roll(down, m, 0), 0.0)
            out[c, i] = total
        return carry

    lax.fori_loop(0, 8, layer, 0)
    factor = (0.25 * COURANT) / jnp.full((16, 256), speed[0], jnp.float32)
    for c in range(5):
        for i in range(8):
            total = out[c, i]
            for m in range(1, 5):
                for j, sign in ((i + m, -1.0), (i - m, 1.0)):
                    if 0 <= j < 8:
                        total = total + (sign * FIRST[m - 1]) * fluxes[c, j]
                        if c:
                            total = total + SECOND[m - 1] * smooths[c - 1, j]
            out[c, i] = 0.75 * start[c, i] + 0.25 * section[c, i] + factor * total


def rim_kernel(speed, inner, y_odd, x_odd, x_even, y_even, out, peak, fluxes, smooths, sums):
    rows = lax.broadcasted_iota(jnp.int32, (8, 256), 0)
    even_first = (rows // 4) == odd("gy")
    below = odd("gx")

    def x_rim(i, carry):
        for k, side in ((1 - below, x_even), (below, x_odd)):
            q = [side[c, i] for c in range(5)]
            inverse, velocity, kinetic, pressure = primitive(q)
            g = smooth(inverse, velocity, kinetic, pressure)
            f = flux(q, velocity, pressure, 0)
            for c in range(5):
                fluxes[k, c, i] = f[c]
                if c:
                    smooths[k, c - 1, i] = g[c]
        return carry

    def y_rim(j, carry):
        for second in range(2):
            q = []
            for c in range(5):
                a, b = (y_odd, y_even) if second else (y_even, y_odd)
                q.append(jnp.where(even_first, a[c, j], b[c, j]))
            inverse, velocity, kinetic, pressure = primitive(q)
            g = smooth(inverse, velocity, kinetic, pressure)
            f = flux(q, velocity, pressure, 1)
            turn = 4 * second
            for c in range(5):
                lower = jnp.zeros((8, 256), jnp.float32)
                upper = jnp.zeros((8, 256), jnp.float32)
                for m in range(1, 5):
                    up, down = sides(f[c], g[c], m)
                    lower = lower + jnp.where(rows < m, pltpu.roll(down, (m + turn) % 8, 0), 0.0)
                    upper = upper + jnp.where(rows >= 8 - m, pltpu.roll(up, (8 - m + turn) % 8, 0), 0.0)
                sums[c, 2 * j + second, 0:8] = lower
                sums[c, 2 * j + second, 8:16] = upper
        return carry

    lax.fori_loop(0, 4, x_rim, 0)
    lax.fori_loop(0, 4, y_rim, 0)
    factor = (0.25 * COURANT) / jnp.full((16, 256), speed[0], jnp.float32)
    most = jnp.zeros((16, 256), jnp.float32)
    for i in range(8):
        new = []
        for c in range(5):
            total = sums[c, i]
            for m in range(1, 5):
                for k, j, sign in ((0, i - m, 1.0), (1, i + m - 8, -1.0)):
                    j = j + 4 if k == 0 else j
                    if (k == 0 and i - m < 0) or (k == 1 and i + m > 7):
                        total = total + (sign * FIRST[m - 1]) * fluxes[k, c, j]
                        if c:
                            total = total + SECOND[m - 1] * smooths[k, c - 1, j]
            value = inner[c, i] + factor * total
            out[c, i] = value
            new.append(value)
        inverse, velocity, kinetic, pressure = primitive(new)
        most = jnp.maximum(most, jnp.sqrt(2.0 * kinetic) + jnp.sqrt(GAMMA * pressure * inverse))
    peak[...] = jnp.full(peak.shape, jnp.max(most), jnp.float32)


def shape(*sizes):
    return jax.ShapeDtypeStruct(sizes, jnp.float32)


def in_vmem(n):
    return [pl.BlockSpec(memory_space=VMEM)] * n


def call(kernel, outs, n_in, scratch, speed, *arrays):
    specs = in_vmem(n_in)
    if speed is not None:
        specs = [pl.BlockSpec(memory_space=SMEM)] + specs
        arrays = (speed,) + arrays
    return pl.pallas_call(
        kernel,
        out_shape=outs,
        in_specs=specs,
        out_specs=tuple(in_vmem(len(outs))),
        scratch_shapes=scratch,
        compiler_params=pltpu.CompilerParams(vmem_limit_bytes=24 << 20),
    )(*arrays)


def swap(x, axis, offset):
    n = lax.axis_size(axis)
    pairs = [((i + offset) % n, (i + 1 + offset) % n) for i in range(0, n, 2)]
    return lax.ppermute(x, axis, pairs + [(b, a) for a, b in pairs])


def local(start, section, previous_speed):
    speed = previous_speed.reshape(1)
    devices = lax.axis_size(("gx", "gy"))
    x_even, x_odd, y_even, y_odd = call(
        pack_kernel,
        (shape(5, 4, 16, 256), shape(5, 4, 16, 256), shape(5, 4, 8, 256), shape(5, 4, 8, 256)),
        1,
        [],
        None,
        start,
    )
    received = (
        swap(y_odd, "gy", 1),
        swap(x_odd, "gx", 1),
        swap(x_even, "gx", 0),
        swap(y_even, "gy", 0),
    )
    (inner,) = call(
        inner_kernel,
        (shape(5, 8, 16, 256),),
        2,
        [VMEM((5, 8, 16, 256), jnp.float32), VMEM((4, 8, 16, 256), jnp.float32)],
        speed,
        start,
        section,
    )
    new, peak = call(
        rim_kernel,
        (shape(5, 8, 16, 256), shape(devices, 128)),
        5,
        [
            VMEM((2, 5, 4, 16, 256), jnp.float32),
            VMEM((2, 4, 4, 16, 256), jnp.float32),
            VMEM((5, 8, 16, 256), jnp.float32),
        ],
        speed,
        inner,
        *received,
    )
    peaks = lax.all_to_all(peak, ("gx", "gy"), 0, 0, tiled=True)
    return new, jnp.max(peaks)


def solution(mesh):
    spec = P(None, "gx", "gy", None)
    return jax.shard_map(
        local, mesh=mesh, in_specs=(spec, spec, P()), out_specs=(spec, P()), check_vma=False
    )
```

```python
import jax
import jax.numpy as jnp
from jax import lax
from jax.experimental import pallas as pl
from jax.experimental.pallas import tpu as pltpu
from jax.sharding import PartitionSpec as P

GAMMA = 1.4
COURANT = 0.3
VISCOSITY = 0.05
CONDUCTION = 0.07
FIRST = (0.8, -0.2, 4.0 / 105.0, -1.0 / 280.0)
SECOND = (1.6, -0.2, 8.0 / 315.0, -1.0 / 560.0)
CENTRE = -205.0 / 72.0
VMEM = pltpu.VMEM
SMEM = pltpu.SMEM
INNER_COST, ODD_COST, EVEN_COST = 1 << 20, 8 << 20, 1 << 20


def primitive(q):
    inverse = 1.0 / q[0]
    u, v, w = q[1] * inverse, q[2] * inverse, q[3] * inverse
    kinetic = 0.5 * (u * u + v * v + w * w)
    pressure = (GAMMA - 1.0) * (q[4] - q[0] * kinetic)
    return inverse, (u, v, w), kinetic, pressure


def flux(q, velocity, pressure, d):
    s = velocity[d]
    out = [q[1 + d], q[1] * s, q[2] * s, q[3] * s, (q[4] + pressure) * s]
    out[1 + d] = out[1 + d] + pressure
    return out


def smooth(inverse, velocity, kinetic, pressure):
    heat = VISCOSITY * kinetic + CONDUCTION * (pressure * inverse)
    return [None] + [VISCOSITY * s for s in velocity] + [heat]


def sides(f, g, m):
    first = FIRST[m - 1] * f
    if g is None:
        return -first, first
    second = SECOND[m - 1] * g
    return second - first, second + first


def odd(axis):
    return lax.rem(lax.axis_index(axis), 2)


def pack_kernel(start, x_odd, y_odd, x_even, y_even):
    side = odd("gx")
    x_even[...] = start[:, pl.ds(4 - 4 * side, 4)]
    x_odd[...] = start[:, pl.ds(4 * side, 4)]
    first = lax.broadcasted_iota(jnp.int32, (8, 256), 0) < 4
    upper = odd("gy") == 0
    for c in range(5):
        for j in range(4):
            a, b = start[c, 2 * j, 0:8], start[c, 2 * j + 1, 0:8]
            low = jnp.where(first, a, pltpu.roll(b, 4, 0))
            a, b = start[c, 2 * j, 8:16], start[c, 2 * j + 1, 8:16]
            high = jnp.where(first, pltpu.roll(b, 4, 0), a)
            y_even[c, j] = jnp.where(upper, high, low)
            y_odd[c, j] = jnp.where(upper, low, high)


def inner_kernel(speed, start, section_far, out, step, section, fluxes, smooths, sems):
    copies = [
        pltpu.make_async_copy(section_far.at[:, i], section.at[:, i], sems.at[i]) for i in range(8)
    ]
    for copy in copies:
        copy.start()
    rows = lax.broadcasted_iota(jnp.int32, (16, 256), 0)

    def layer(i, carry):
        pltpu.make_async_copy(section_far.at[:, i], section.at[:, i], sems.at[i]).wait()
        q = [section[c, i] for c in range(5)]
        inverse, velocity, kinetic, pressure = primitive(q)
        g = smooth(inverse, velocity, kinetic, pressure)
        fx = flux(q, velocity, pressure, 0)
        fy = flux(q, velocity, pressure, 1)
        fz = flux(q, velocity, pressure, 2)
        for c in range(5):
            fluxes[c, i] = fx[c]
            total = jnp.zeros((16, 256), jnp.float32)
            if c:
                smooths[c - 1, i] = g[c]
                total = (3.0 * CENTRE) * g[c]
            for m in range(1, 5):
                up, down = sides(fz[c], g[c], m)
                total = total + pltpu.roll(up, 256 - m, 1) + pltpu.roll(down, m, 1)
                up, down = sides(fy[c], g[c], m)
                total = total + jnp.where(rows < 16 - m, pltpu.roll(up, 16 - m, 0), 0.0)
                total = total + jnp.where(rows >= m, pltpu.roll(down, m, 0), 0.0)
            out[c, i] = total
        return carry

    lax.fori_loop(0, 8, layer, 0)
    factor = (0.25 * COURANT) / jnp.broadcast_to(speed[...], (8, 128))
    step[...] = factor
    factor = jnp.tile(factor, (2, 2))
    for c in range(5):
        for i in range(8):
            total = out[c, i]
            for m in range(1, 5):
                for j, sign in ((i + m, -1.0), (i - m, 1.0)):
                    if 0 <= j < 8:
                        total = total + (sign * FIRST[m - 1]) * fluxes[c, j]
                        if c:
                            total = total + SECOND[m - 1] * smooths[c - 1, j]
            out[c, i] = 0.75 * start[c, i] + 0.25 * section[c, i] + factor * total


def y_side(rim, sums, below):
    rows = lax.broadcasted_iota(jnp.int32, (8, 256), 0)

    def pair(j, carry):
        q = [rim[c, j] for c in range(5)]
        inverse, velocity, kinetic, pressure = primitive(q)
        g = smooth(inverse, velocity, kinetic, pressure)
        f = flux(q, velocity, pressure, 1)
        for c in range(5):
            totals = [None, None]
            for m in range(1, 5):
                up, down = sides(f[c], g[c], m)
                for second in range(2):
                    if below:
                        part = jnp.where(rows < m, pltpu.roll(down, (m + 4 * second) % 8, 0), 0.0)
                    else:
                        part = jnp.where(rows >= 8 - m, pltpu.roll(up, (8 - m + 4 * second) % 8, 0), 0.0)
                    totals[second] = part if totals[second] is None else totals[second] + part
            sums[c, 2 * j] = totals[0]
            sums[c, 2 * j + 1] = totals[1]
        return carry

    lax.fori_loop(0, 4, pair, 0)


def rim_terms(x_below, y_below, x_rim, y_rim, fluxes, smooths, sums):
    @pl.when(y_below == 1)
    def _():
        y_side(y_rim, sums, True)

    @pl.when(y_below == 0)
    def _():
        y_side(y_rim, sums, False)

    sign = jnp.where(x_below == 1, 1.0, -1.0)

    def x_layer(d, carry):
        i = jnp.where(x_below == 1, 3 - d, d)
        q = [x_rim[c, i] for c in range(5)]
        inverse, velocity, kinetic, pressure = primitive(q)
        g = smooth(inverse, velocity, kinetic, pressure)
        f = flux(q, velocity, pressure, 0)
        for c in range(5):
            fluxes[c, d] = sign * f[c]
            if c:
                smooths[c - 1, d] = g[c]
        return carry

    lax.fori_loop(0, 4, x_layer, 0)


def rim_layer(t, x_below, y_below, inner, step, fluxes, smooths, sums):
    i = jnp.where(x_below == 1, t, 7 - t)
    factor = jnp.tile(step[...], (1, 2))
    low = jnp.where(y_below == 1, factor, 0.0)
    edge = jnp.concatenate([low, factor - low], axis=0)
    factor = jnp.concatenate([factor, factor], axis=0)
    values = []
    for c in range(5):
        part = sums[c, i]
        value = inner[c, i] + edge * jnp.concatenate([part, part], axis=0)
        total = None
        for d in range(4 - t):
            term = FIRST[d + t] * fluxes[c, d]
            if c:
                term = term + SECOND[d + t] * smooths[c - 1, d]
            total = term if total is None else total + term
        if total is not None:
            value = value + factor * total
        values.append(value)
    return i, values


def odd_kernel(inner, step, x_rim, y_rim, out, fluxes, smooths, sums):
    x_below, y_below = 1 - odd("gx"), 1 - odd("gy")
    rim_terms(x_below, y_below, x_rim, y_rim, fluxes, smooths, sums)
    for t in range(8):
        i, values = rim_layer(t, x_below, y_below, inner, step, fluxes, smooths, sums)
        for c in range(5):
            out[c, i] = values[c]


def even_kernel(inner, step, x_rim, y_rim, out, peak, fluxes, smooths, sums):
    x_below, y_below = odd("gx"), odd("gy")
    rim_terms(x_below, y_below, x_rim, y_rim, fluxes, smooths, sums)
    most = None
    for t in range(8):
        i, values = rim_layer(t, x_below, y_below, inner, step, fluxes, smooths, sums)
        for c in range(5):
            out[c, i] = values[c]
        inverse, velocity, kinetic, pressure = primitive(values)
        speed = jnp.sqrt(2.0 * kinetic) + jnp.sqrt(GAMMA * pressure * inverse)
        most = speed if most is None else jnp.maximum(most, speed)
    peak[...] = jnp.full(peak.shape, jnp.max(most), jnp.float32)


def most_kernel(peaks, out):
    out[0] = jnp.max(peaks[...])


def in_vmem(*sizes):
    return VMEM(sizes, jnp.float32)


def call(kernel, outs, in_specs, scratch, cost, *arrays, out_space=VMEM):
    estimate = pl.CostEstimate(flops=cost * 300, bytes_accessed=cost, transcendentals=0) if cost else None
    return pl.pallas_call(
        kernel,
        out_shape=outs,
        in_specs=[pl.BlockSpec(memory_space=m) for m in in_specs],
        out_specs=tuple(pl.BlockSpec(memory_space=out_space) for _ in outs),
        scratch_shapes=scratch,
        cost_estimate=estimate,
        compiler_params=pltpu.CompilerParams(vmem_limit_bytes=24 << 20),
    )(*arrays)


def far(x):
    return pltpu.with_memory_space_constraint(x, pltpu.HBM)


def swap(x, axis, offset):
    n = lax.axis_size(axis)
    pairs = [((i + offset) % n, (i + 1 + offset) % n) for i in range(0, n, 2)]
    return lax.ppermute(x, axis, pairs + [(b, a) for a, b in pairs])


def local(start, section, previous_speed):
    devices = lax.axis_size(("gx", "gy"))
    x_odd, y_odd, x_even, y_even = call(
        pack_kernel,
        (in_vmem(5, 4, 16, 256), in_vmem(5, 4, 8, 256)) * 2,
        [VMEM],
        [],
        0,
        start,
    )
    x_odd, y_odd = swap(x_odd, "gx", 1), swap(y_odd, "gy", 1)
    y_even, x_even = swap(y_even, "gy", 0), swap(x_even, "gx", 0)
    state = in_vmem(5, 8, 16, 256)
    inner, step = call(
        inner_kernel,
        (state, in_vmem(8, 128)),
        [VMEM, VMEM, pltpu.HBM],
        [
            state,
            state,
            in_vmem(4, 8, 16, 256),
            pltpu.SemaphoreType.DMA((8,)),
        ],
        INNER_COST,
        previous_speed.reshape(1, 1),
        start,
        far(section),
    )
    rims = [in_vmem(5, 4, 16, 256), in_vmem(4, 4, 16, 256), in_vmem(5, 8, 8, 256)]
    (inner,) = call(odd_kernel, (state,), [VMEM] * 4, rims, ODD_COST, inner, step, x_odd, y_odd)
    new, peak = call(
        even_kernel,
        (state, in_vmem(devices, 128)),
        [VMEM] * 4,
        rims,
        EVEN_COST,
        inner,
        step,
        x_even,
        y_even,
    )
    peaks = lax.all_to_all(peak, ("gx", "gy"), 0, 0, tiled=True)
    (most,) = call(
        most_kernel, (SMEM((1,), jnp.float32),), [VMEM], [], 0, peaks, out_space=SMEM
    )
    return new, most.reshape(())


def solution(mesh):
    spec = P(None, "gx", "gy", None)
    return jax.shard_map(
        local, mesh=mesh, in_specs=(spec, spec, P()), out_specs=(spec, P()), check_vma=False
    )
```

```python
import jax
import jax.numpy as jnp
from jax import lax
from jax.experimental import pallas as pl
from jax.experimental.pallas import tpu as pltpu
from jax.sharding import Mesh
from jax.sharding import PartitionSpec as P

GAMMA = 1.4
COURANT = 0.3
VISCOSITY = 0.05
CONDUCTION = 0.07
FIRST = (0.8, -0.2, 4.0 / 105.0, -1.0 / 280.0)
SECOND = (1.6, -0.2, 8.0 / 315.0, -1.0 / 560.0)
CENTRE = -205.0 / 72.0
AXES = ("z_lo", "y", "z_hi", "x", "core")
SIZES = (4, 8, 2, 4, 2)
GX, GY = AXES[:2], AXES[2:]
NEAR, FAR = ("y", "core"), ("z_lo", "z_hi", "x")
VMEM = pltpu.VMEM
SMEM = pltpu.SMEM
INNER_COST, ODD_COST, EVEN_COST = 1 << 20, 8 << 20, 1 << 20


def primitive(q):
    inverse = 1.0 / q[0]
    u, v, w = q[1] * inverse, q[2] * inverse, q[3] * inverse
    kinetic = 0.5 * (u * u + v * v + w * w)
    pressure = (GAMMA - 1.0) * (q[4] - q[0] * kinetic)
    return inverse, (u, v, w), kinetic, pressure


def flux(q, velocity, pressure, d):
    s = velocity[d]
    out = [q[1 + d], q[1] * s, q[2] * s, q[3] * s, (q[4] + pressure) * s]
    out[1 + d] = out[1 + d] + pressure
    return out


def smooth(inverse, velocity, kinetic, pressure):
    heat = VISCOSITY * kinetic + CONDUCTION * (pressure * inverse)
    return [None] + [VISCOSITY * s for s in velocity] + [heat]


def sides(f, g, m):
    first = FIRST[m - 1] * f
    if g is None:
        return -first, first
    second = SECOND[m - 1] * g
    return second - first, second + first


def odd(axis):
    return lax.rem(lax.axis_index(axis), 2)


def pack_kernel(far_start, x_odd, y_odd, x_even, y_even, start, sems):
    copies = [
        pltpu.make_async_copy(far_start.at[c, rows], start.at[c, rows], sems.at[c, k])
        for c in range(5)
        for k, rows in enumerate((pl.ds(0, 4), pl.ds(4, 4)))
    ]
    for copy in copies:
        copy.start()
    side = odd("y")
    first = lax.broadcasted_iota(jnp.int32, (8, 256), 0) < 4
    upper = odd("core") == 0
    for c in range(5):
        copies[2 * c].wait()
        copies[2 * c + 1].wait()
        x_even[c] = start[c, pl.ds(4 - 4 * side, 4)]
        x_odd[c] = start[c, pl.ds(4 * side, 4)]
        for j in range(4):
            a, b = start[c, 2 * j, 0:8], start[c, 2 * j + 1, 0:8]
            low = jnp.where(first, a, pltpu.roll(b, 4, 0))
            a, b = start[c, 2 * j, 8:16], start[c, 2 * j + 1, 8:16]
            high = jnp.where(first, pltpu.roll(b, 4, 0), a)
            y_even[c, j] = jnp.where(upper, high, low)
            y_odd[c, j] = jnp.where(upper, low, high)


def inner_kernel(speed, start, section_far, out, step, section, fluxes, smooths, sems):
    copies = [
        pltpu.make_async_copy(section_far.at[:, i], section.at[:, i], sems.at[i]) for i in range(8)
    ]
    for copy in copies:
        copy.start()
    rows = lax.broadcasted_iota(jnp.int32, (16, 256), 0)

    def layer(i, carry):
        pltpu.make_async_copy(section_far.at[:, i], section.at[:, i], sems.at[i]).wait()
        q = [section[c, i] for c in range(5)]
        inverse, velocity, kinetic, pressure = primitive(q)
        g = smooth(inverse, velocity, kinetic, pressure)
        fx = flux(q, velocity, pressure, 0)
        fy = flux(q, velocity, pressure, 1)
        fz = flux(q, velocity, pressure, 2)
        for c in range(5):
            fluxes[c, i] = fx[c]
            total = jnp.zeros((16, 256), jnp.float32)
            if c:
                smooths[c - 1, i] = g[c]
                total = (3.0 * CENTRE) * g[c]
            for m in range(1, 5):
                up, down = sides(fz[c], g[c], m)
                total = total + pltpu.roll(up, 256 - m, 1) + pltpu.roll(down, m, 1)
                up, down = sides(fy[c], g[c], m)
                total = total + jnp.where(rows < 16 - m, pltpu.roll(up, 16 - m, 0), 0.0)
                total = total + jnp.where(rows >= m, pltpu.roll(down, m, 0), 0.0)
            out[c, i] = total
        return carry

    lax.fori_loop(0, 8, layer, 0)
    factor = (0.25 * COURANT) / jnp.broadcast_to(speed[...], (8, 128))
    step[...] = factor
    factor = jnp.tile(factor, (2, 2))
    for c in range(5):
        for i in range(8):
            total = out[c, i]
            for m in range(1, 5):
                for j, sign in ((i + m, -1.0), (i - m, 1.0)):
                    if 0 <= j < 8:
                        total = total + (sign * FIRST[m - 1]) * fluxes[c, j]
                        if c:
                            total = total + SECOND[m - 1] * smooths[c - 1, j]
            out[c, i] = 0.75 * start[c, i] + 0.25 * section[c, i] + factor * total


def y_side(rim, sums, below):
    rows = lax.broadcasted_iota(jnp.int32, (8, 256), 0)

    def pair(j, carry):
        q = [rim[c, j] for c in range(5)]
        inverse, velocity, kinetic, pressure = primitive(q)
        g = smooth(inverse, velocity, kinetic, pressure)
        f = flux(q, velocity, pressure, 1)
        for c in range(5):
            totals = [None, None]
            for m in range(1, 5):
                up, down = sides(f[c], g[c], m)
                for second in range(2):
                    if below:
                        part = jnp.where(rows < m, pltpu.roll(down, (m + 4 * second) % 8, 0), 0.0)
                    else:
                        part = jnp.where(rows >= 8 - m, pltpu.roll(up, (8 - m + 4 * second) % 8, 0), 0.0)
                    totals[second] = part if totals[second] is None else totals[second] + part
            sums[c, 2 * j] = totals[0]
            sums[c, 2 * j + 1] = totals[1]
        return carry

    lax.fori_loop(0, 4, pair, 0)


def rim_terms(x_below, y_below, x_rim, y_rim, fluxes, smooths, sums):
    @pl.when(y_below == 1)
    def _():
        y_side(y_rim, sums, True)

    @pl.when(y_below == 0)
    def _():
        y_side(y_rim, sums, False)

    sign = jnp.where(x_below == 1, 1.0, -1.0)

    def x_layer(d, carry):
        i = jnp.where(x_below == 1, 3 - d, d)
        q = [x_rim[c, i] for c in range(5)]
        inverse, velocity, kinetic, pressure = primitive(q)
        g = smooth(inverse, velocity, kinetic, pressure)
        f = flux(q, velocity, pressure, 0)
        for c in range(5):
            fluxes[c, d] = sign * f[c]
            if c:
                smooths[c - 1, d] = g[c]
        return carry

    lax.fori_loop(0, 4, x_layer, 0)


def rim_layer(t, x_below, y_below, inner, step, fluxes, smooths, sums):
    i = jnp.where(x_below == 1, t, 7 - t)
    factor = jnp.tile(step[...], (1, 2))
    low = jnp.where(y_below == 1, factor, 0.0)
    edge = jnp.concatenate([low, factor - low], axis=0)
    factor = jnp.concatenate([factor, factor], axis=0)
    values = []
    for c in range(5):
        part = sums[c, i]
        value = inner[c, i] + edge * jnp.concatenate([part, part], axis=0)
        total = None
        for d in range(4 - t):
            term = FIRST[d + t] * fluxes[c, d]
            if c:
                term = term + SECOND[d + t] * smooths[c - 1, d]
            total = term if total is None else total + term
        if total is not None:
            value = value + factor * total
        values.append(value)
    return i, values


def odd_kernel(inner, step, x_rim, y_rim, out, fluxes, smooths, sums):
    x_below, y_below = 1 - odd("y"), 1 - odd("core")
    rim_terms(x_below, y_below, x_rim, y_rim, fluxes, smooths, sums)
    for t in range(8):
        i, values = rim_layer(t, x_below, y_below, inner, step, fluxes, smooths, sums)
        for c in range(5):
            out[c, i] = values[c]


def even_kernel(inner, step, x_rim, y_rim, out, peak, fluxes, smooths, sums):
    x_below, y_below = odd("y"), odd("core")
    rim_terms(x_below, y_below, x_rim, y_rim, fluxes, smooths, sums)
    most = None
    for t in range(8):
        i, values = rim_layer(t, x_below, y_below, inner, step, fluxes, smooths, sums)
        for c in range(5):
            out[c, i] = values[c]
        inverse, velocity, kinetic, pressure = primitive(values)
        speed = jnp.sqrt(2.0 * kinetic) + jnp.sqrt(GAMMA * pressure * inverse)
        most = speed if most is None else jnp.maximum(most, speed)
    most = jnp.maximum(most[:, :128], most[:, 128:])
    spread(most, peak)


def spread(values, out):
    out[...] = jnp.broadcast_to(jnp.max(values, axis=0, keepdims=True), out.shape)


def pass_kernel(peaks, out):
    spread(peaks[...], out)


def most_kernel(peaks, out):
    out[0] = jnp.max(peaks[...])


def in_vmem(*sizes):
    return VMEM(sizes, jnp.float32)


def call(kernel, outs, in_specs, scratch, cost, *arrays, out_space=VMEM):
    estimate = pl.CostEstimate(flops=cost * 300, bytes_accessed=cost, transcendentals=0) if cost else None
    return pl.pallas_call(
        kernel,
        out_shape=outs,
        in_specs=[pl.BlockSpec(memory_space=m) for m in in_specs],
        out_specs=tuple(pl.BlockSpec(memory_space=out_space) for _ in outs),
        scratch_shapes=scratch,
        cost_estimate=estimate,
        compiler_params=pltpu.CompilerParams(vmem_limit_bytes=24 << 20),
    )(*arrays)


def far(x):
    return pltpu.with_memory_space_constraint(x, pltpu.HBM)


def swap(x, axis, offset):
    n = lax.axis_size(axis)
    pairs = [((i + offset) % n, (i + 1 + offset) % n) for i in range(0, n, 2)]
    return lax.ppermute(x, axis, pairs + [(b, a) for a, b in pairs])


def local(start, section, previous_speed):
    x_odd, y_odd, x_even, y_even = call(
        pack_kernel,
        (in_vmem(5, 4, 16, 256), in_vmem(5, 4, 8, 256)) * 2,
        [pltpu.HBM],
        [in_vmem(5, 8, 16, 256), pltpu.SemaphoreType.DMA((5, 2))],
        0,
        far(start),
    )
    x_odd, y_odd = swap(x_odd, GX, 1), swap(y_odd, GY, 1)
    y_even, x_even = swap(y_even, GY, 0), swap(x_even, GX, 0)
    state = in_vmem(5, 8, 16, 256)
    inner, step = call(
        inner_kernel,
        (state, in_vmem(8, 128)),
        [VMEM, VMEM, pltpu.HBM],
        [
            state,
            state,
            in_vmem(4, 8, 16, 256),
            pltpu.SemaphoreType.DMA((8,)),
        ],
        INNER_COST,
        previous_speed.reshape(1, 1),
        start,
        far(section),
    )
    rims = [in_vmem(5, 4, 16, 256), in_vmem(4, 4, 16, 256), in_vmem(5, 8, 8, 256)]
    (inner,) = call(odd_kernel, (state,), [VMEM] * 4, rims, ODD_COST, inner, step, x_odd, y_odd)
    new, peak = call(
        even_kernel,
        (state, in_vmem(lax.axis_size(NEAR), 128)),
        [VMEM] * 4,
        rims,
        EVEN_COST,
        inner,
        step,
        x_even,
        y_even,
    )
    peaks = lax.all_to_all(peak, NEAR, 0, 0, tiled=True)
    (peak,) = call(pass_kernel, (in_vmem(lax.axis_size(FAR), 128),), [VMEM], [], 0, peaks)
    peaks = lax.all_to_all(peak, FAR, 0, 0, tiled=True)
    (most,) = call(
        most_kernel, (SMEM((1,), jnp.float32),), [VMEM], [], 0, peaks, out_space=SMEM
    )
    return new, most.reshape(())


def solution(mesh):
    split = Mesh(mesh.devices.reshape(SIZES), AXES)
    spec = P(None, GX, GY, None)
    return jax.shard_map(
        local, mesh=split, in_specs=(spec, spec, P()), out_specs=(spec, P()), check_vma=False
    )
```

```python
import jax
import jax.numpy as jnp
from jax import lax
from jax.experimental import pallas as pl
from jax.experimental.pallas import tpu as pltpu
from jax.sharding import Mesh
from jax.sharding import PartitionSpec as P

GAMMA = 1.4
COURANT = 0.3
VISCOSITY = 0.05
CONDUCTION = 0.07
FIRST = (0.8, -0.2, 4.0 / 105.0, -1.0 / 280.0)
SECOND = (1.6, -0.2, 8.0 / 315.0, -1.0 / 560.0)
CENTRE = -205.0 / 72.0
AXES = ("z_lo", "y", "z_hi", "x", "core")
SIZES = (4, 8, 2, 4, 2)
GX, GY = AXES[:2], AXES[2:]
NEAR, FAR = ("y", "core"), ("z_lo", "z_hi", "x")
VMEM = pltpu.VMEM
SMEM = pltpu.SMEM
INNER_COST, ODD_COST, EVEN_COST = 1 << 20, 8 << 20, 1 << 20


def primitive(q):
    inverse = 1.0 / q[0]
    u, v, w = q[1] * inverse, q[2] * inverse, q[3] * inverse
    kinetic = 0.5 * (u * u + v * v + w * w)
    pressure = (GAMMA - 1.0) * (q[4] - q[0] * kinetic)
    return inverse, (u, v, w), kinetic, pressure


def flux(q, velocity, pressure, d):
    s = velocity[d]
    out = [q[1 + d], q[1] * s, q[2] * s, q[3] * s, (q[4] + pressure) * s]
    out[1 + d] = out[1 + d] + pressure
    return out


def smooth(inverse, velocity, kinetic, pressure):
    heat = VISCOSITY * kinetic + CONDUCTION * (pressure * inverse)
    return [None] + [VISCOSITY * s for s in velocity] + [heat]


def sides(f, g, m):
    first = FIRST[m - 1] * f
    if g is None:
        return -first, first
    second = SECOND[m - 1] * g
    return second - first, second + first


def odd(axis):
    return lax.rem(lax.axis_index(axis), 2)


def early():
    return (lax.axis_index("z_hi") == 0) & (lax.axis_index("z_lo") < 3)


def inner_work(start, section_far, base, rate, section, fluxes, smooths, sems):
    def copy(i):
        return pltpu.make_async_copy(section_far.at[:, i], section.at[:, i], sems.at[i])

    for i in range(8):
        copy(i).start()
    rows = lax.broadcasted_iota(jnp.int32, (16, 256), 0)

    def layer(i, carry):
        copy(i).wait()
        q = [section[c, i] for c in range(5)]
        inverse, velocity, kinetic, pressure = primitive(q)
        g = smooth(inverse, velocity, kinetic, pressure)
        fx = flux(q, velocity, pressure, 0)
        fy = flux(q, velocity, pressure, 1)
        fz = flux(q, velocity, pressure, 2)
        for c in range(5):
            fluxes[c, i] = fx[c]
            base[c, i] = 0.75 * start[c, i] + 0.25 * q[c]
            total = jnp.zeros((16, 256), jnp.float32)
            if c:
                smooths[c - 1, i] = g[c]
                total = (3.0 * CENTRE) * g[c]
            for m in range(1, 5):
                up, down = sides(fz[c], g[c], m)
                total = total + pltpu.roll(up, 256 - m, 1) + pltpu.roll(down, m, 1)
                up, down = sides(fy[c], g[c], m)
                total = total + jnp.where(rows < 16 - m, pltpu.roll(up, 16 - m, 0), 0.0)
                total = total + jnp.where(rows >= m, pltpu.roll(down, m, 0), 0.0)
            rate[c, i] = total
        return carry

    lax.fori_loop(0, 8, layer, 0)
    for c in range(5):
        for i in range(8):
            total = rate[c, i]
            for m in range(1, 5):
                for j, sign in ((i + m, -1.0), (i - m, 1.0)):
                    if 0 <= j < 8:
                        total = total + (sign * FIRST[m - 1]) * fluxes[c, j]
                        if c:
                            total = total + SECOND[m - 1] * smooths[c - 1, j]
            rate[c, i] = total


def pack_kernel(far_start, section_far, x_odd, y_odd, x_even, y_even, start, rate, sems, *work):
    copies = [
        pltpu.make_async_copy(far_start.at[c, rows], start.at[c, rows], sems.at[c, k])
        for c in range(5)
        for k, rows in enumerate((pl.ds(0, 4), pl.ds(4, 4)))
    ]
    for copy in copies:
        copy.start()
    side = odd("y")
    first = lax.broadcasted_iota(jnp.int32, (8, 256), 0) < 4
    upper = odd("core") == 0
    for c in range(5):
        copies[2 * c].wait()
        copies[2 * c + 1].wait()
        x_even[c] = start[c, pl.ds(4 - 4 * side, 4)]
        x_odd[c] = start[c, pl.ds(4 * side, 4)]
        for j in range(4):
            a, b = start[c, 2 * j, 0:8], start[c, 2 * j + 1, 0:8]
            low = jnp.where(first, a, pltpu.roll(b, 4, 0))
            a, b = start[c, 2 * j, 8:16], start[c, 2 * j + 1, 8:16]
            high = jnp.where(first, pltpu.roll(b, 4, 0), a)
            y_even[c, j] = jnp.where(upper, high, low)
            y_odd[c, j] = jnp.where(upper, low, high)

    @pl.when(early())
    def _():
        inner_work(start, section_far, start, rate, *work)


def inner_kernel(speed, start, section_far, early_rate, step, base, rate, *work):
    step[...] = (0.25 * COURANT) / jnp.broadcast_to(speed[...], (8, 128))

    @pl.when(early())
    def _():
        base[...] = start[...]
        rate[...] = early_rate[...]

    @pl.when(jnp.logical_not(early()))
    def _():
        inner_work(start, section_far, base, rate, *work)


def y_side(rim, sums, below):
    rows = lax.broadcasted_iota(jnp.int32, (8, 256), 0)

    def pair(j, carry):
        q = [rim[c, j] for c in range(5)]
        inverse, velocity, kinetic, pressure = primitive(q)
        g = smooth(inverse, velocity, kinetic, pressure)
        f = flux(q, velocity, pressure, 1)
        for c in range(5):
            totals = [None, None]
            for m in range(1, 5):
                up, down = sides(f[c], g[c], m)
                for second in range(2):
                    if below:
                        part = jnp.where(rows < m, pltpu.roll(down, (m + 4 * second) % 8, 0), 0.0)
                    else:
                        part = jnp.where(rows >= 8 - m, pltpu.roll(up, (8 - m + 4 * second) % 8, 0), 0.0)
                    totals[second] = part if totals[second] is None else totals[second] + part
            sums[c, 2 * j] = totals[0]
            sums[c, 2 * j + 1] = totals[1]
        return carry

    lax.fori_loop(0, 4, pair, 0)


def rim_terms(x_below, y_below, x_rim, y_rim, fluxes, smooths, sums):
    @pl.when(y_below == 1)
    def _():
        y_side(y_rim, sums, True)

    @pl.when(y_below == 0)
    def _():
        y_side(y_rim, sums, False)

    sign = jnp.where(x_below == 1, 1.0, -1.0)

    def x_layer(d, carry):
        i = jnp.where(x_below == 1, 3 - d, d)
        q = [x_rim[c, i] for c in range(5)]
        inverse, velocity, kinetic, pressure = primitive(q)
        g = smooth(inverse, velocity, kinetic, pressure)
        f = flux(q, velocity, pressure, 0)
        for c in range(5):
            fluxes[c, d] = sign * f[c]
            if c:
                smooths[c - 1, d] = g[c]
        return carry

    lax.fori_loop(0, 4, x_layer, 0)


def rim_layer(t, x_below, y_below, base, rate, step, fluxes, smooths, sums):
    i = jnp.where(x_below == 1, t, 7 - t)
    factor = jnp.tile(step[...], (1, 2))
    low = jnp.where(y_below == 1, factor, 0.0)
    edge = jnp.concatenate([low, factor - low], axis=0)
    factor = jnp.concatenate([factor, factor], axis=0)
    values = []
    for c in range(5):
        part = sums[c, i]
        value = base[c, i] + edge * jnp.concatenate([part, part], axis=0)
        total = None if rate is None else rate[c, i]
        for d in range(4 - t):
            term = FIRST[d + t] * fluxes[c, d]
            if c:
                term = term + SECOND[d + t] * smooths[c - 1, d]
            total = term if total is None else total + term
        if total is not None:
            value = value + factor * total
        values.append(value)
    return i, values


def odd_kernel(base, rate, step, x_rim, y_rim, out, fluxes, smooths, sums):
    x_below, y_below = 1 - odd("y"), 1 - odd("core")
    rim_terms(x_below, y_below, x_rim, y_rim, fluxes, smooths, sums)
    for t in range(8):
        i, values = rim_layer(t, x_below, y_below, base, rate, step, fluxes, smooths, sums)
        for c in range(5):
            out[c, i] = values[c]


def even_kernel(base, step, x_rim, y_rim, out, peak, fluxes, smooths, sums):
    x_below, y_below = odd("y"), odd("core")
    rim_terms(x_below, y_below, x_rim, y_rim, fluxes, smooths, sums)
    most = None
    for t in range(8):
        i, values = rim_layer(t, x_below, y_below, base, None, step, fluxes, smooths, sums)
        for c in range(5):
            out[c, i] = values[c]
        inverse, velocity, kinetic, pressure = primitive(values)
        speed = jnp.sqrt(2.0 * kinetic) + jnp.sqrt(GAMMA * pressure * inverse)
        most = speed if most is None else jnp.maximum(most, speed)
    most = jnp.maximum(most[:, :128], most[:, 128:])
    spread(most, peak)


def spread(values, out):
    out[...] = jnp.broadcast_to(jnp.max(values, axis=0, keepdims=True), out.shape)


def pass_kernel(peaks, out):
    spread(peaks[...], out)


def most_kernel(peaks, out):
    out[0] = jnp.max(peaks[...])


def in_vmem(*sizes):
    return VMEM(sizes, jnp.float32)


def call(kernel, outs, in_specs, scratch, cost, *arrays, out_space=VMEM):
    estimate = pl.CostEstimate(flops=cost * 300, bytes_accessed=cost, transcendentals=0) if cost else None
    return pl.pallas_call(
        kernel,
        out_shape=outs,
        in_specs=[pl.BlockSpec(memory_space=m) for m in in_specs],
        out_specs=tuple(pl.BlockSpec(memory_space=out_space) for _ in outs),
        scratch_shapes=scratch,
        cost_estimate=estimate,
        compiler_params=pltpu.CompilerParams(vmem_limit_bytes=8 << 20),
    )(*arrays)


def far(x):
    return pltpu.with_memory_space_constraint(x, pltpu.HBM)


def swap(x, axis, offset):
    n = lax.axis_size(axis)
    pairs = [((i + offset) % n, (i + 1 + offset) % n) for i in range(0, n, 2)]
    return lax.ppermute(x, axis, pairs + [(b, a) for a, b in pairs])


def local(start, section, previous_speed):
    state = in_vmem(5, 8, 16, 256)
    work = [state, state, in_vmem(4, 8, 16, 256), pltpu.SemaphoreType.DMA((8,))]
    x_odd, y_odd, x_even, y_even, start, rate = call(
        pack_kernel,
        (in_vmem(5, 4, 16, 256), in_vmem(5, 4, 8, 256)) * 2 + (state,) * 2,
        [pltpu.HBM] * 2,
        [pltpu.SemaphoreType.DMA((5, 2))] + work,
        0,
        far(start),
        far(section),
    )
    x_odd, y_odd = swap(x_odd, GX, 1), swap(y_odd, GY, 1)
    y_even, x_even = swap(y_even, GY, 0), swap(x_even, GX, 0)
    step, base, rate = call(
        inner_kernel,
        (in_vmem(8, 128), state, state),
        [VMEM, VMEM, pltpu.HBM, VMEM],
        work,
        INNER_COST,
        previous_speed.reshape(1, 1),
        start,
        far(section),
        rate,
    )
    rims = [in_vmem(5, 4, 16, 256), in_vmem(4, 4, 16, 256), in_vmem(5, 8, 8, 256)]
    (base,) = call(
        odd_kernel, (state,), [VMEM] * 5, rims, ODD_COST, base, rate, step, x_odd, y_odd
    )
    new, peak = call(
        even_kernel,
        (state, in_vmem(lax.axis_size(NEAR), 128)),
        [VMEM] * 4,
        rims,
        EVEN_COST,
        base,
        step,
        x_even,
        y_even,
    )
    peaks = lax.all_to_all(peak, NEAR, 0, 0, tiled=True)
    (peak,) = call(pass_kernel, (in_vmem(lax.axis_size(FAR), 128),), [VMEM], [], 0, peaks)
    peaks = lax.all_to_all(peak, FAR, 0, 0, tiled=True)
    (most,) = call(
        most_kernel, (SMEM((1,), jnp.float32),), [VMEM], [], 0, peaks, out_space=SMEM
    )
    return new, most.reshape(())


def solution(mesh):
    split = Mesh(mesh.devices.reshape(SIZES), AXES)
    spec = P(None, GX, GY, None)
    return jax.shard_map(
        local, mesh=split, in_specs=(spec, spec, P()), out_specs=(spec, P()), check_vma=False
    )
```

```python
import jax
import jax.numpy as jnp
from jax import lax
from jax.experimental import pallas as pl
from jax.experimental.pallas import tpu as pltpu
from jax.sharding import Mesh
from jax.sharding import PartitionSpec as P

GAMMA = 1.4
COURANT = 0.3
VISCOSITY = 0.05
CONDUCTION = 0.07
FIRST = (0.8, -0.2, 4.0 / 105.0, -1.0 / 280.0)
SECOND = (1.6, -0.2, 8.0 / 315.0, -1.0 / 560.0)
CENTRE = -205.0 / 72.0
AXES = ("z_lo", "y", "z_hi", "x", "core")
SIZES = (4, 8, 2, 4, 2)
GX, GY = AXES[:2], AXES[2:]
NEAR, FAR = ("y", "core"), ("z_lo", "z_hi", "x")
VMEM = pltpu.VMEM
SMEM = pltpu.SMEM
INNER_COST, ODD_COST, EVEN_COST = 1 << 20, 1 << 18, 1 << 20
Y_COST = 7 << 20


def primitive(q):
    inverse = 1.0 / q[0]
    u, v, w = q[1] * inverse, q[2] * inverse, q[3] * inverse
    kinetic = 0.5 * (u * u + v * v + w * w)
    pressure = (GAMMA - 1.0) * (q[4] - q[0] * kinetic)
    return inverse, (u, v, w), kinetic, pressure


def flux(q, velocity, pressure, d):
    s = velocity[d]
    out = [q[1 + d], q[1] * s, q[2] * s, q[3] * s, (q[4] + pressure) * s]
    out[1 + d] = out[1 + d] + pressure
    return out


def smooth(inverse, velocity, kinetic, pressure):
    heat = VISCOSITY * kinetic + CONDUCTION * (pressure * inverse)
    return [None] + [VISCOSITY * s for s in velocity] + [heat]


def sides(f, g, m):
    first = FIRST[m - 1] * f
    if g is None:
        return -first, first
    second = SECOND[m - 1] * g
    return second - first, second + first


def odd(axis):
    return lax.rem(lax.axis_index(axis), 2)


def early():
    return (lax.axis_index("z_hi") == 0) & (lax.axis_index("z_lo") < 3)


def inner_work(start, section_far, base, rate, section, fluxes, smooths, sems):
    def copy(i):
        return pltpu.make_async_copy(section_far.at[:, i], section.at[:, i], sems.at[i])

    for i in range(8):
        copy(i).start()
    rows = lax.broadcasted_iota(jnp.int32, (16, 256), 0)

    def layer(i, carry):
        copy(i).wait()
        q = [section[c, i] for c in range(5)]
        inverse, velocity, kinetic, pressure = primitive(q)
        g = smooth(inverse, velocity, kinetic, pressure)
        fx = flux(q, velocity, pressure, 0)
        fy = flux(q, velocity, pressure, 1)
        fz = flux(q, velocity, pressure, 2)
        for c in range(5):
            fluxes[c, i] = fx[c]
            base[c, i] = 0.75 * start[c, i] + 0.25 * q[c]
            total = jnp.zeros((16, 256), jnp.float32)
            if c:
                smooths[c - 1, i] = g[c]
                total = (3.0 * CENTRE) * g[c]
            for m in range(1, 5):
                up, down = sides(fz[c], g[c], m)
                total = total + pltpu.roll(up, 256 - m, 1) + pltpu.roll(down, m, 1)
                up, down = sides(fy[c], g[c], m)
                total = total + jnp.where(rows < 16 - m, pltpu.roll(up, 16 - m, 0), 0.0)
                total = total + jnp.where(rows >= m, pltpu.roll(down, m, 0), 0.0)
            rate[c, i] = total
        return carry

    lax.fori_loop(0, 8, layer, 0)
    for c in range(5):
        for i in range(8):
            total = rate[c, i]
            for m in range(1, 5):
                for j, sign in ((i + m, -1.0), (i - m, 1.0)):
                    if 0 <= j < 8:
                        total = total + (sign * FIRST[m - 1]) * fluxes[c, j]
                        if c:
                            total = total + SECOND[m - 1] * smooths[c - 1, j]
            rate[c, i] = total


def pack_kernel(far_start, section_far, x_odd, y_odd, x_even, y_even, start, rate, sems, *work):
    copies = [
        pltpu.make_async_copy(far_start.at[c, rows], start.at[c, rows], sems.at[c, k])
        for c in range(5)
        for k, rows in enumerate((pl.ds(0, 4), pl.ds(4, 4)))
    ]
    for copy in copies:
        copy.start()
    side = odd("y")
    first = lax.broadcasted_iota(jnp.int32, (8, 256), 0) < 4
    upper = odd("core") == 0
    for c in range(5):
        copies[2 * c].wait()
        copies[2 * c + 1].wait()
        x_even[c] = start[c, pl.ds(4 - 4 * side, 4)]
        x_odd[c] = start[c, pl.ds(4 * side, 4)]
        for j in range(4):
            a, b = start[c, 2 * j, 0:8], start[c, 2 * j + 1, 0:8]
            low = jnp.where(first, a, pltpu.roll(b, 4, 0))
            a, b = start[c, 2 * j, 8:16], start[c, 2 * j + 1, 8:16]
            high = jnp.where(first, pltpu.roll(b, 4, 0), a)
            y_even[c, j] = jnp.where(upper, high, low)
            y_odd[c, j] = jnp.where(upper, low, high)

    @pl.when(early())
    def _():
        inner_work(start, section_far, start, rate, *work)


def inner_kernel(speed, start, section_far, early_rate, step, base, rate, *work):
    step[...] = (0.25 * COURANT) / jnp.broadcast_to(speed[...], (8, 128))

    @pl.when(early())
    def _():
        base[...] = start[...]
        rate[...] = early_rate[...]

    @pl.when(jnp.logical_not(early()))
    def _():
        inner_work(start, section_far, base, rate, *work)


def y_side(rim, sums, below):
    rows = lax.broadcasted_iota(jnp.int32, (8, 256), 0)

    def pair(j, carry):
        q = [rim[c, j] for c in range(5)]
        inverse, velocity, kinetic, pressure = primitive(q)
        g = smooth(inverse, velocity, kinetic, pressure)
        f = flux(q, velocity, pressure, 1)
        for c in range(5):
            totals = [None, None]
            for m in range(1, 5):
                up, down = sides(f[c], g[c], m)
                for second in range(2):
                    if below:
                        part = jnp.where(rows < m, pltpu.roll(down, (m + 4 * second) % 8, 0), 0.0)
                    else:
                        part = jnp.where(rows >= 8 - m, pltpu.roll(up, (8 - m + 4 * second) % 8, 0), 0.0)
                    totals[second] = part if totals[second] is None else totals[second] + part
            sums[c, 2 * j] = totals[0]
            sums[c, 2 * j + 1] = totals[1]
        return carry

    lax.fori_loop(0, 4, pair, 0)


def x_side(x_rim, below, fluxes, smooths):
    sign = jnp.where(below == 1, 1.0, -1.0)

    def layer(d, carry):
        i = jnp.where(below == 1, 3 - d, d)
        q = [x_rim[c, i] for c in range(5)]
        inverse, velocity, kinetic, pressure = primitive(q)
        g = smooth(inverse, velocity, kinetic, pressure)
        f = flux(q, velocity, pressure, 0)
        for c in range(5):
            fluxes[c, d] = sign * f[c]
            if c:
                smooths[c - 1, d] = g[c]
        return carry

    lax.fori_loop(0, 4, layer, 0)


def finish(below, base, rate, step, fluxes, smooths, new, out, sems):
    factor = jnp.tile(step[...], (2, 2))
    most = None
    copies = []
    for t in range(4):
        i = jnp.where(below == 1, t, 7 - t)
        values = []
        for c in range(5):
            total = None if rate is None else rate[c, i]
            for d in range(4 - t):
                term = FIRST[d + t] * fluxes[c, d]
                if c:
                    term = term + SECOND[d + t] * smooths[c - 1, d]
                total = term if total is None else total + term
            value = base[c, i] + factor * total
            new[c, t] = value
            values.append(value)
        copy = pltpu.make_async_copy(new.at[:, t], out.at[:, i], sems.at[t])
        copy.start()
        copies.append(copy)
        inverse, velocity, kinetic, pressure = primitive(values)
        speed = jnp.sqrt(2.0 * kinetic) + jnp.sqrt(GAMMA * pressure * inverse)
        most = speed if most is None else jnp.maximum(most, speed)
    most = jnp.maximum(most[:, :128], most[:, 128:])
    return copies, jnp.maximum(most[:8], most[8:])


def one_side(rim, below, sums):
    for side, rows, others in ((1, pl.ds(0, 8), pl.ds(8, 8)), (0, pl.ds(8, 8), pl.ds(0, 8))):

        @pl.when(below == side)
        def _(side=side, rows=rows, others=others):
            y_side(rim, sums.at[:, :, rows], side == 1)
            sums[:, :, others] = jnp.zeros((5, 8, 8, 256), jnp.float32)


def y_kernel(rate, rim, out, sums):
    one_side(rim, 1 - odd("core"), sums)
    out[...] = rate[...] + sums[...]


def odd_kernel(base, rate, step, x_rim, y_even, out, rest, most, fluxes, smooths, sums, new, sems):
    below = 1 - odd("y")
    one_side(y_even, odd("core"), sums)
    factor = jnp.tile(step[...], (2, 2))

    def layer(t, carry):
        i = jnp.where(below == 1, 7 - t, t)
        for c in range(5):
            rest[c, i] = base[c, i] + factor * (rate[c, i] + sums[c, i])
        return carry

    def edge(t, carry):
        i = jnp.where(below == 1, t, 7 - t)
        for c in range(5):
            sums[c, i] = sums[c, i] + rate[c, i]
        return carry

    x_side(x_rim, below, fluxes, smooths)
    lax.fori_loop(0, 4, edge, 0)
    copies, most[...] = finish(below, base, sums, step, fluxes, smooths, new, out, sems)
    lax.fori_loop(0, 4, layer, 0)
    for copy in copies:
        copy.wait()


def even_kernel(rest, step, most, x_rim, half, out, peak, fluxes, smooths, new, sems):
    below = odd("y")
    x_side(x_rim, below, fluxes, smooths)
    copies, mine = finish(below, rest, None, step, fluxes, smooths, new, out, sems)
    spread(jnp.maximum(mine, most[...]), peak)
    for copy in copies:
        copy.wait()


def spread(values, out):
    out[...] = jnp.broadcast_to(jnp.max(values, axis=0, keepdims=True), out.shape)


def pass_kernel(peaks, out):
    spread(peaks[...], out)


def most_kernel(peaks, out):
    out[0] = jnp.max(peaks[...])


def in_vmem(*sizes):
    return VMEM(sizes, jnp.float32)


def call(kernel, outs, in_specs, scratch, cost, *arrays, out_specs=None, aliases=None):
    estimate = pl.CostEstimate(flops=cost * 300, bytes_accessed=cost, transcendentals=0) if cost else None
    return pl.pallas_call(
        kernel,
        out_shape=outs,
        in_specs=[pl.BlockSpec(memory_space=m) for m in in_specs],
        out_specs=tuple(pl.BlockSpec(memory_space=m) for m in out_specs or (VMEM,) * len(outs)),
        scratch_shapes=scratch,
        cost_estimate=estimate,
        input_output_aliases=aliases or {},
        compiler_params=pltpu.CompilerParams(vmem_limit_bytes=8 << 20),
    )(*arrays)


def far(x):
    return pltpu.with_memory_space_constraint(x, pltpu.HBM)


def swap(x, axis, offset):
    n = lax.axis_size(axis)
    pairs = [((i + offset) % n, (i + 1 + offset) % n) for i in range(0, n, 2)]
    return lax.ppermute(x, axis, pairs + [(b, a) for a, b in pairs])


def local(start, section, previous_speed):
    state = in_vmem(5, 8, 16, 256)
    work = [state, state, in_vmem(4, 8, 16, 256), pltpu.SemaphoreType.DMA((8,))]
    x_odd, y_odd, x_even, y_even, start, rate = call(
        pack_kernel,
        (in_vmem(5, 4, 16, 256), in_vmem(5, 4, 8, 256)) * 2 + (state,) * 2,
        [pltpu.HBM] * 2,
        [pltpu.SemaphoreType.DMA((5, 2))] + work,
        0,
        far(start),
        far(section),
    )
    x_odd, y_odd = swap(x_odd, GX, 1), swap(y_odd, GY, 1)
    y_even, x_even = swap(y_even, GY, 0), swap(x_even, GX, 0)
    step, base, rate = call(
        inner_kernel,
        (in_vmem(8, 128), state, state),
        [VMEM, VMEM, pltpu.HBM, VMEM],
        work,
        INNER_COST,
        previous_speed.reshape(1, 1),
        start,
        far(section),
        rate,
    )
    rims = [in_vmem(5, 4, 16, 256), in_vmem(4, 4, 16, 256)]
    outgoing = [in_vmem(5, 4, 16, 256), pltpu.SemaphoreType.DMA((4,))]
    far_state = pltpu.HBM((5, 8, 16, 256), jnp.float32)
    (rate,) = call(y_kernel, (state,), [VMEM] * 2, [state], Y_COST, rate, y_odd)
    half, rest, most = call(
        odd_kernel,
        (far_state, state, in_vmem(8, 128)),
        [VMEM] * 5,
        rims + [state] + outgoing,
        ODD_COST,
        base,
        rate,
        step,
        x_odd,
        y_even,
        out_specs=(pltpu.HBM, VMEM, VMEM),
    )
    new, peak = call(
        even_kernel,
        (far_state, in_vmem(lax.axis_size(NEAR), 128)),
        [VMEM] * 4 + [pltpu.HBM],
        rims + outgoing,
        EVEN_COST,
        rest,
        step,
        most,
        x_even,
        half,
        out_specs=(pltpu.HBM, VMEM),
        aliases={4: 0},
    )
    peaks = lax.all_to_all(peak, NEAR, 0, 0, tiled=True)
    (peak,) = call(pass_kernel, (in_vmem(lax.axis_size(FAR), 128),), [VMEM], [], 0, peaks)
    peaks = lax.all_to_all(peak, FAR, 0, 0, tiled=True)
    (most,) = call(
        most_kernel, (SMEM((1,), jnp.float32),), [VMEM], [], 0, peaks, out_specs=(SMEM,)
    )
    return new, most.reshape(())


def solution(mesh):
    split = Mesh(mesh.devices.reshape(SIZES), AXES)
    spec = P(None, GX, GY, None)
    return jax.shard_map(
        local, mesh=split, in_specs=(spec, spec, P()), out_specs=(spec, P()), check_vma=False
    )
```

```python
import jax
import jax.numpy as jnp
from jax import lax
from jax.experimental import pallas as pl
from jax.experimental.pallas import tpu as pltpu
from jax.sharding import Mesh
from jax.sharding import PartitionSpec as P

GAMMA = 1.4
COURANT = 0.3
VISCOSITY = 0.05
CONDUCTION = 0.07
FIRST = (0.8, -0.2, 4.0 / 105.0, -1.0 / 280.0)
SECOND = (1.6, -0.2, 8.0 / 315.0, -1.0 / 560.0)
CENTRE = -205.0 / 72.0
AXES = ("z_lo", "y", "z_hi", "x", "core")
SIZES = (4, 8, 2, 4, 2)
GX, GY = AXES[:2], AXES[2:]
NEAR, FAR = ("y", "core"), ("z_lo", "z_hi", "x")
VMEM = pltpu.VMEM
SMEM = pltpu.SMEM
INNER_COST, ODD_COST, EVEN_COST = 1 << 20, 3 << 20, 1 << 20
Y_COST = 4 << 20


def primitive(q):
    inverse = 1.0 / q[0]
    u, v, w = q[1] * inverse, q[2] * inverse, q[3] * inverse
    kinetic = 0.5 * (u * u + v * v + w * w)
    pressure = (GAMMA - 1.0) * (q[4] - q[0] * kinetic)
    return inverse, (u, v, w), kinetic, pressure


def flux(q, velocity, pressure, d):
    s = velocity[d]
    out = [q[1 + d], q[1] * s, q[2] * s, q[3] * s, (q[4] + pressure) * s]
    out[1 + d] = out[1 + d] + pressure
    return out


def smooth(inverse, velocity, kinetic, pressure):
    heat = VISCOSITY * kinetic + CONDUCTION * (pressure * inverse)
    return [None] + [VISCOSITY * s for s in velocity] + [heat]


def sides(f, g, m):
    first = FIRST[m - 1] * f
    if g is None:
        return -first, first
    second = SECOND[m - 1] * g
    return second - first, second + first


def odd(axis):
    return lax.rem(lax.axis_index(axis), 2)


def early():
    return (lax.axis_index("z_hi") == 0) & (lax.axis_index("z_lo") < 3)


def inner_work(start, section_far, base, rate, section, fluxes, smooths, sems):
    def copy(i):
        return pltpu.make_async_copy(section_far.at[:, i], section.at[:, i], sems.at[i])

    for i in range(8):
        copy(i).start()
    rows = lax.broadcasted_iota(jnp.int32, (16, 256), 0)

    def layer(i, carry):
        copy(i).wait()
        q = [section[c, i] for c in range(5)]
        inverse, velocity, kinetic, pressure = primitive(q)
        g = smooth(inverse, velocity, kinetic, pressure)
        fx = flux(q, velocity, pressure, 0)
        fy = flux(q, velocity, pressure, 1)
        fz = flux(q, velocity, pressure, 2)
        for c in range(5):
            fluxes[c, i] = fx[c]
            base[c, i] = 0.75 * start[c, i] + 0.25 * q[c]
            total = jnp.zeros((16, 256), jnp.float32)
            if c:
                smooths[c - 1, i] = g[c]
                total = (3.0 * CENTRE) * g[c]
            for m in range(1, 5):
                up, down = sides(fz[c], g[c], m)
                total = total + pltpu.roll(up, 256 - m, 1) + pltpu.roll(down, m, 1)
                up, down = sides(fy[c], g[c], m)
                total = total + jnp.where(rows < 16 - m, pltpu.roll(up, 16 - m, 0), 0.0)
                total = total + jnp.where(rows >= m, pltpu.roll(down, m, 0), 0.0)
            rate[c, i] = total
        return carry

    lax.fori_loop(0, 8, layer, 0)
    for c in range(5):
        for i in range(8):
            total = rate[c, i]
            for m in range(1, 5):
                for j, sign in ((i + m, -1.0), (i - m, 1.0)):
                    if 0 <= j < 8:
                        total = total + (sign * FIRST[m - 1]) * fluxes[c, j]
                        if c:
                            total = total + SECOND[m - 1] * smooths[c - 1, j]
            rate[c, i] = total


def pack_kernel(far_start, section_far, x_odd, y_odd, x_even, y_even, start, rate, sems, *work):
    copies = [
        pltpu.make_async_copy(far_start.at[c, rows], start.at[c, rows], sems.at[c, k])
        for c in range(5)
        for k, rows in enumerate((pl.ds(0, 4), pl.ds(4, 4)))
    ]
    for copy in copies:
        copy.start()
    side = odd("y")
    first = lax.broadcasted_iota(jnp.int32, (8, 256), 0) < 4
    upper = odd("core") == 0
    for c in range(5):
        copies[2 * c].wait()
        copies[2 * c + 1].wait()
        x_even[c] = start[c, pl.ds(4 - 4 * side, 4)]
        x_odd[c] = start[c, pl.ds(4 * side, 4)]
        for j in range(4):
            a, b = start[c, 2 * j, 0:8], start[c, 2 * j + 1, 0:8]
            low = jnp.where(first, a, pltpu.roll(b, 4, 0))
            a, b = start[c, 2 * j, 8:16], start[c, 2 * j + 1, 8:16]
            high = jnp.where(first, pltpu.roll(b, 4, 0), a)
            y_even[c, j] = jnp.where(upper, high, low)
            y_odd[c, j] = jnp.where(upper, low, high)

    @pl.when(early())
    def _():
        inner_work(start, section_far, start, rate, *work)


def inner_kernel(speed, start, section_far, early_rate, step, base, rate, *work):
    step[...] = (0.25 * COURANT) / jnp.broadcast_to(speed[...], (8, 128))

    @pl.when(early())
    def _():
        base[...] = start[...]
        rate[...] = early_rate[...]

    @pl.when(jnp.logical_not(early()))
    def _():
        inner_work(start, section_far, base, rate, *work)


def y_side(rim, sums, below):
    rows = lax.broadcasted_iota(jnp.int32, (8, 256), 0)

    def pair(j, carry):
        q = [rim[c, j] for c in range(5)]
        inverse, velocity, kinetic, pressure = primitive(q)
        g = smooth(inverse, velocity, kinetic, pressure)
        f = flux(q, velocity, pressure, 1)
        for c in range(5):
            totals = [None, None]
            for m in range(1, 5):
                up, down = sides(f[c], g[c], m)
                for second in range(2):
                    if below:
                        part = jnp.where(rows < m, pltpu.roll(down, (m + 4 * second) % 8, 0), 0.0)
                    else:
                        part = jnp.where(rows >= 8 - m, pltpu.roll(up, (8 - m + 4 * second) % 8, 0), 0.0)
                    totals[second] = part if totals[second] is None else totals[second] + part
            sums[c, 2 * j] = totals[0]
            sums[c, 2 * j + 1] = totals[1]
        return carry

    lax.fori_loop(0, 4, pair, 0)


def x_side(x_rim, below, fluxes, smooths):
    sign = jnp.where(below == 1, 1.0, -1.0)

    def layer(d, carry):
        i = jnp.where(below == 1, 3 - d, d)
        q = [x_rim[c, i] for c in range(5)]
        inverse, velocity, kinetic, pressure = primitive(q)
        g = smooth(inverse, velocity, kinetic, pressure)
        f = flux(q, velocity, pressure, 0)
        for c in range(5):
            fluxes[c, d] = sign * f[c]
            if c:
                smooths[c - 1, d] = g[c]
        return carry

    lax.fori_loop(0, 4, layer, 0)


def finish(below, base, rate, step, fluxes, smooths, new, out, sems):
    factor = jnp.tile(step[...], (2, 2))
    most = None
    copies = []
    for t in range(4):
        i = jnp.where(below == 1, t, 7 - t)
        values = []
        for c in range(5):
            total = None if rate is None else rate[c, i]
            for d in range(4 - t):
                term = FIRST[d + t] * fluxes[c, d]
                if c:
                    term = term + SECOND[d + t] * smooths[c - 1, d]
                total = term if total is None else total + term
            value = base[c, i] + factor * total
            new[c, t] = value
            values.append(value)
        copy = pltpu.make_async_copy(new.at[:, t], out.at[:, i], sems.at[t])
        copy.start()
        copies.append(copy)
        inverse, velocity, kinetic, pressure = primitive(values)
        speed = jnp.sqrt(2.0 * kinetic) + jnp.sqrt(GAMMA * pressure * inverse)
        most = speed if most is None else jnp.maximum(most, speed)
    most = jnp.maximum(most[:, :128], most[:, 128:])
    return copies, jnp.maximum(most[:8], most[8:])


def one_side(rim, below, sums):
    for side, rows, others in ((1, pl.ds(0, 8), pl.ds(8, 8)), (0, pl.ds(8, 8), pl.ds(0, 8))):

        @pl.when(below == side)
        def _(side=side, rows=rows, others=others):
            y_side(rim, sums.at[:, :, rows], side == 1)
            sums[:, :, others] = jnp.zeros((5, 8, 8, 256), jnp.float32)


def y_kernel(rate, rim, out, sums):
    one_side(rim, 1 - odd("core"), sums)
    out[...] = rate[...] + sums[...]


def odd_kernel(base, rate, step, x_rim, y_even, out, rest, most, fluxes, smooths, sums, new, sems):
    below = 1 - odd("y")
    one_side(y_even, odd("core"), sums)
    factor = jnp.tile(step[...], (2, 2))

    def layer(t, carry):
        i = jnp.where(below == 1, 7 - t, t)
        for c in range(5):
            rest[c, i] = base[c, i] + factor * (rate[c, i] + sums[c, i])
        return carry

    def edge(t, carry):
        i = jnp.where(below == 1, t, 7 - t)
        for c in range(5):
            sums[c, i] = sums[c, i] + rate[c, i]
        return carry

    x_side(x_rim, below, fluxes, smooths)
    lax.fori_loop(0, 4, edge, 0)
    copies, most[...] = finish(below, base, sums, step, fluxes, smooths, new, out, sems)
    lax.fori_loop(0, 4, layer, 0)
    for copy in copies:
        copy.wait()


def even_kernel(rest, step, most, x_rim, half, out, peak, fluxes, smooths, new, sems):
    below = odd("y")
    x_side(x_rim, below, fluxes, smooths)
    copies, mine = finish(below, rest, None, step, fluxes, smooths, new, out, sems)
    spread(jnp.maximum(mine, most[...]), peak)
    for copy in copies:
        copy.wait()


def spread(values, out):
    out[...] = jnp.broadcast_to(jnp.max(values, axis=0, keepdims=True), out.shape)


def pass_kernel(peaks, out):
    spread(peaks[...], out)


def most_kernel(peaks, out):
    out[0] = jnp.max(peaks[...])


def in_vmem(*sizes):
    return VMEM(sizes, jnp.float32)


def call(kernel, outs, in_specs, scratch, cost, *arrays, out_specs=None, aliases=None):
    estimate = pl.CostEstimate(flops=cost * 300, bytes_accessed=cost, transcendentals=0) if cost else None
    return pl.pallas_call(
        kernel,
        out_shape=outs,
        in_specs=[pl.BlockSpec(memory_space=m) for m in in_specs],
        out_specs=tuple(pl.BlockSpec(memory_space=m) for m in out_specs or (VMEM,) * len(outs)),
        scratch_shapes=scratch,
        cost_estimate=estimate,
        input_output_aliases=aliases or {},
        compiler_params=pltpu.CompilerParams(vmem_limit_bytes=8 << 20),
    )(*arrays)


def far(x):
    return pltpu.with_memory_space_constraint(x, pltpu.HBM)


def swap(x, axis, offset):
    n = lax.axis_size(axis)
    pairs = [((i + offset) % n, (i + 1 + offset) % n) for i in range(0, n, 2)]
    return lax.ppermute(x, axis, pairs + [(b, a) for a, b in pairs])


def local(start, section, previous_speed):
    state = in_vmem(5, 8, 16, 256)
    work = [state, state, in_vmem(4, 8, 16, 256), pltpu.SemaphoreType.DMA((8,))]
    x_odd, y_odd, x_even, y_even, start, rate = call(
        pack_kernel,
        (in_vmem(5, 4, 16, 256), in_vmem(5, 4, 8, 256)) * 2 + (state,) * 2,
        [pltpu.HBM] * 2,
        [pltpu.SemaphoreType.DMA((5, 2))] + work,
        0,
        far(start),
        far(section),
    )
    x_odd, y_odd = swap(x_odd, GX, 1), swap(y_odd, GY, 1)
    y_even, x_even = swap(y_even, GY, 0), swap(x_even, GX, 0)
    step, base, rate = call(
        inner_kernel,
        (in_vmem(8, 128), state, state),
        [VMEM, VMEM, pltpu.HBM, VMEM],
        work,
        INNER_COST,
        previous_speed.reshape(1, 1),
        start,
        far(section),
        rate,
    )
    rims = [in_vmem(5, 4, 16, 256), in_vmem(4, 4, 16, 256)]
    outgoing = [in_vmem(5, 4, 16, 256), pltpu.SemaphoreType.DMA((4,))]
    far_state = pltpu.HBM((5, 8, 16, 256), jnp.float32)
    (rate,) = call(y_kernel, (state,), [VMEM] * 2, [state], Y_COST, rate, y_odd)
    half, rest, most = call(
        odd_kernel,
        (far_state, state, in_vmem(8, 128)),
        [VMEM] * 5,
        rims + [state] + outgoing,
        ODD_COST,
        base,
        rate,
        step,
        x_odd,
        y_even,
        out_specs=(pltpu.HBM, VMEM, VMEM),
    )
    new, peak = call(
        even_kernel,
        (far_state, in_vmem(lax.axis_size(NEAR), 128)),
        [VMEM] * 4 + [pltpu.HBM],
        rims + outgoing,
        EVEN_COST,
        rest,
        step,
        most,
        x_even,
        half,
        out_specs=(pltpu.HBM, VMEM),
        aliases={4: 0},
    )
    peaks = lax.all_to_all(peak, NEAR, 0, 0, tiled=True)
    (peak,) = call(pass_kernel, (in_vmem(lax.axis_size(FAR), 128),), [VMEM], [], 0, peaks)
    peaks = lax.all_to_all(peak, FAR, 0, 0, tiled=True)
    (most,) = call(
        most_kernel, (SMEM((1,), jnp.float32),), [VMEM], [], 0, peaks, out_specs=(SMEM,)
    )
    return new, most.reshape(())


def solution(mesh):
    split = Mesh(mesh.devices.reshape(SIZES), AXES)
    spec = P(None, GX, GY, None)
    return jax.shard_map(
        local, mesh=split, in_specs=(spec, spec, P()), out_specs=(spec, P()), check_vma=False
    )
```

```python
import jax
import jax.numpy as jnp
from jax import lax
from jax.experimental import pallas as pl
from jax.experimental.pallas import tpu as pltpu
from jax.sharding import Mesh
from jax.sharding import PartitionSpec as P

GAMMA = 1.4
COURANT = 0.3
VISCOSITY = 0.05
CONDUCTION = 0.07
FIRST = (0.8, -0.2, 4.0 / 105.0, -1.0 / 280.0)
SECOND = (1.6, -0.2, 8.0 / 315.0, -1.0 / 560.0)
CENTRE = -205.0 / 72.0
AXES = ("z_lo", "y", "z_hi", "x", "core")
SIZES = (4, 8, 2, 4, 2)
GX, GY = AXES[:2], AXES[2:]
VMEM = pltpu.VMEM
SMEM = pltpu.SMEM
INNER_COST, X_COST, Y_COST, LAST_COST = 1 << 20, 1 << 20, 7 << 20, 1 << 20


def primitive(q):
    inverse = 1.0 / q[0]
    u, v, w = q[1] * inverse, q[2] * inverse, q[3] * inverse
    kinetic = 0.5 * (u * u + v * v + w * w)
    pressure = (GAMMA - 1.0) * (q[4] - q[0] * kinetic)
    return inverse, (u, v, w), kinetic, pressure


def flux(q, velocity, pressure, d):
    s = velocity[d]
    out = [q[1 + d], q[1] * s, q[2] * s, q[3] * s, (q[4] + pressure) * s]
    out[1 + d] = out[1 + d] + pressure
    return out


def smooth(inverse, velocity, kinetic, pressure):
    heat = VISCOSITY * kinetic + CONDUCTION * (pressure * inverse)
    return [None] + [VISCOSITY * s for s in velocity] + [heat]


def sides(f, g, m):
    first = FIRST[m - 1] * f
    if g is None:
        return -first, first
    second = SECOND[m - 1] * g
    return second - first, second + first


def odd(axis):
    return lax.rem(lax.axis_index(axis), 2)


def early():
    return (lax.axis_index("z_hi") == 0) & (lax.axis_index("z_lo") < 3)


def inner_work(start, section_far, base, rate, section, fluxes, smooths, sems):
    def copy(i):
        return pltpu.make_async_copy(section_far.at[:, i], section.at[:, i], sems.at[i])

    for i in range(8):
        copy(i).start()
    rows = lax.broadcasted_iota(jnp.int32, (16, 256), 0)

    def layer(i, carry):
        copy(i).wait()
        q = [section[c, i] for c in range(5)]
        inverse, velocity, kinetic, pressure = primitive(q)
        g = smooth(inverse, velocity, kinetic, pressure)
        fx = flux(q, velocity, pressure, 0)
        fy = flux(q, velocity, pressure, 1)
        fz = flux(q, velocity, pressure, 2)
        for c in range(5):
            fluxes[c, i] = fx[c]
            base[c, i] = 0.75 * start[c, i] + 0.25 * q[c]
            total = jnp.zeros((16, 256), jnp.float32)
            if c:
                smooths[c - 1, i] = g[c]
                total = (3.0 * CENTRE) * g[c]
            for m in range(1, 5):
                up, down = sides(fz[c], g[c], m)
                total = total + pltpu.roll(up, 256 - m, 1) + pltpu.roll(down, m, 1)
                up, down = sides(fy[c], g[c], m)
                total = total + jnp.where(rows < 16 - m, pltpu.roll(up, 16 - m, 0), 0.0)
                total = total + jnp.where(rows >= m, pltpu.roll(down, m, 0), 0.0)
            rate[c, i] = total
        return carry

    lax.fori_loop(0, 8, layer, 0)
    for c in range(5):
        for i in range(8):
            total = rate[c, i]
            for m in range(1, 5):
                for j, sign in ((i + m, -1.0), (i - m, 1.0)):
                    if 0 <= j < 8:
                        total = total + (sign * FIRST[m - 1]) * fluxes[c, j]
                        if c:
                            total = total + SECOND[m - 1] * smooths[c - 1, j]
            rate[c, i] = total


def pack_kernel(far_start, section_far, x_odd, y_odd, x_even, y_even, start, rate, sems, *work):
    copies = [
        pltpu.make_async_copy(far_start.at[c, rows], start.at[c, rows], sems.at[c, k])
        for c in range(5)
        for k, rows in enumerate((pl.ds(0, 4), pl.ds(4, 4)))
    ]
    for copy in copies:
        copy.start()
    side = odd("y")
    first = lax.broadcasted_iota(jnp.int32, (8, 256), 0) < 4
    upper = odd("core") == 0
    for c in range(5):
        copies[2 * c].wait()
        copies[2 * c + 1].wait()
        x_even[c] = start[c, pl.ds(4 - 4 * side, 4)]
        x_odd[c] = start[c, pl.ds(4 * side, 4)]
        for j in range(4):
            a, b = start[c, 2 * j, 0:8], start[c, 2 * j + 1, 0:8]
            low = jnp.where(first, a, pltpu.roll(b, 4, 0))
            a, b = start[c, 2 * j, 8:16], start[c, 2 * j + 1, 8:16]
            high = jnp.where(first, pltpu.roll(b, 4, 0), a)
            y_even[c, j] = jnp.where(upper, high, low)
            y_odd[c, j] = jnp.where(upper, low, high)

    @pl.when(early())
    def _():
        inner_work(start, section_far, start, rate, *work)


def inner_kernel(speed, start, section_far, early_rate, step, base, rate, *work):
    step[...] = (0.25 * COURANT) / jnp.broadcast_to(speed[...], (8, 128))

    @pl.when(early())
    def _():
        base[...] = start[...]
        rate[...] = early_rate[...]

    @pl.when(jnp.logical_not(early()))
    def _():
        inner_work(start, section_far, base, rate, *work)


def y_side(rim, sums, below):
    rows = lax.broadcasted_iota(jnp.int32, (8, 256), 0)

    def pair(j, carry):
        q = [rim[c, j] for c in range(5)]
        inverse, velocity, kinetic, pressure = primitive(q)
        g = smooth(inverse, velocity, kinetic, pressure)
        f = flux(q, velocity, pressure, 1)
        for c in range(5):
            totals = [None, None]
            for m in range(1, 5):
                up, down = sides(f[c], g[c], m)
                for second in range(2):
                    if below:
                        part = jnp.where(rows < m, pltpu.roll(down, (m + 4 * second) % 8, 0), 0.0)
                    else:
                        part = jnp.where(rows >= 8 - m, pltpu.roll(up, (8 - m + 4 * second) % 8, 0), 0.0)
                    totals[second] = part if totals[second] is None else totals[second] + part
            sums[c, 2 * j] = totals[0]
            sums[c, 2 * j + 1] = totals[1]
        return carry

    lax.fori_loop(0, 4, pair, 0)


def x_side(x_rim, below, fluxes, smooths):
    sign = jnp.where(below == 1, 1.0, -1.0)

    def layer(d, carry):
        i = jnp.where(below == 1, 3 - d, d)
        q = [x_rim[c, i] for c in range(5)]
        inverse, velocity, kinetic, pressure = primitive(q)
        g = smooth(inverse, velocity, kinetic, pressure)
        f = flux(q, velocity, pressure, 0)
        for c in range(5):
            fluxes[c, d] = sign * f[c]
            if c:
                smooths[c - 1, d] = g[c]
        return carry

    lax.fori_loop(0, 4, layer, 0)


def x_terms(c, t, fluxes, smooths):
    total = None
    for d in range(4 - t):
        term = FIRST[d + t] * fluxes[c, d]
        if c:
            term = term + SECOND[d + t] * smooths[c - 1, d]
        total = term if total is None else total + term
    return total


def one_side(rim, below, sums):
    for side, rows, others in ((1, pl.ds(0, 8), pl.ds(8, 8)), (0, pl.ds(8, 8), pl.ds(0, 8))):

        @pl.when(below == side)
        def _(side=side, rows=rows, others=others):
            y_side(rim, sums.at[:, :, rows], side == 1)
            sums[:, :, others] = jnp.zeros((5, 8, 8, 256), jnp.float32)


def y_kernel(rate, rim, out, sums):
    one_side(rim, 1 - odd("core"), sums)
    out[...] = rate[...] + sums[...]


def x_kernel(rate, rim, out, fluxes, smooths):
    below = 1 - odd("y")
    x_side(rim, below, fluxes, smooths)
    for t in range(8):
        i = jnp.where(below == 1, t, 7 - t)
        for c in range(5):
            out[c, i] = rate[c, i] + x_terms(c, t, fluxes, smooths) if t < 4 else rate[c, i]


def last_kernel(base, rate, step, x_rim, y_rim, out, peak, fluxes, smooths, sums, new, sems):
    below = odd("y")
    one_side(y_rim, odd("core"), sums)
    x_side(x_rim, below, fluxes, smooths)
    factor = jnp.tile(step[...], (2, 2))
    most = None
    copies = []
    for t in range(7, -1, -1):
        i = jnp.where(below == 1, t, 7 - t)
        values = []
        for c in range(5):
            total = rate[c, i] + sums[c, i]
            if t < 4:
                total = total + x_terms(c, t, fluxes, smooths)
            value = base[c, i] + factor * total
            new[c, t] = value
            values.append(value)
        copy = pltpu.make_async_copy(new.at[:, t], out.at[:, i], sems.at[t])
        copy.start()
        copies.append(copy)
        inverse, velocity, kinetic, pressure = primitive(values)
        speed = jnp.sqrt(2.0 * kinetic) + jnp.sqrt(GAMMA * pressure * inverse)
        most = speed if most is None else jnp.maximum(most, speed)
    spread(jnp.maximum(most[:, :128], most[:, 128:]), peak)
    for copy in copies:
        copy.wait()


def spread(values, out):
    out[...] = jnp.broadcast_to(jnp.max(values, axis=0, keepdims=True), out.shape)


def most_kernel(peaks, out):
    out[0] = jnp.max(peaks[...])


def in_vmem(*sizes):
    return VMEM(sizes, jnp.float32)


def call(kernel, outs, in_specs, scratch, cost, *arrays, out_specs=None, aliases=None):
    estimate = pl.CostEstimate(flops=cost * 300, bytes_accessed=cost, transcendentals=0) if cost else None
    return pl.pallas_call(
        kernel,
        out_shape=outs,
        in_specs=[pl.BlockSpec(memory_space=m) for m in in_specs],
        out_specs=tuple(pl.BlockSpec(memory_space=m) for m in out_specs or (VMEM,) * len(outs)),
        scratch_shapes=scratch,
        cost_estimate=estimate,
        input_output_aliases=aliases or {},
        compiler_params=pltpu.CompilerParams(vmem_limit_bytes=8 << 20),
    )(*arrays)


def far(x):
    return pltpu.with_memory_space_constraint(x, pltpu.HBM)


def swap(x, axis, offset):
    n = lax.axis_size(axis)
    pairs = [((i + offset) % n, (i + 1 + offset) % n) for i in range(0, n, 2)]
    return lax.ppermute(x, axis, pairs + [(b, a) for a, b in pairs])


def local(start, section, previous_speed):
    state = in_vmem(5, 8, 16, 256)
    work = [state, state, in_vmem(4, 8, 16, 256), pltpu.SemaphoreType.DMA((8,))]
    x_odd, y_odd, x_even, y_even, start, rate = call(
        pack_kernel,
        (in_vmem(5, 4, 16, 256), in_vmem(5, 4, 8, 256)) * 2 + (state,) * 2,
        [pltpu.HBM] * 2,
        [pltpu.SemaphoreType.DMA((5, 2))] + work,
        0,
        far(start),
        far(section),
    )
    x_odd, y_odd = swap(x_odd, GX, 1), swap(y_odd, GY, 1)
    y_even, x_even = swap(y_even, GY, 0), swap(x_even, GX, 0)
    step, base, rate = call(
        inner_kernel,
        (in_vmem(8, 128), state, state),
        [VMEM, VMEM, pltpu.HBM, VMEM],
        work,
        INNER_COST,
        previous_speed.reshape(1, 1),
        start,
        far(section),
        rate,
    )
    rims = [in_vmem(5, 4, 16, 256), in_vmem(4, 4, 16, 256)]
    (rate,) = call(x_kernel, (state,), [VMEM] * 2, rims, X_COST, rate, x_odd)
    (rate,) = call(y_kernel, (state,), [VMEM] * 2, [state], Y_COST, rate, y_odd)
    new, peak = call(
        last_kernel,
        (pltpu.HBM((5, 8, 16, 256), jnp.float32), in_vmem(lax.axis_size(AXES), 128)),
        [VMEM] * 5,
        rims + [state, state, pltpu.SemaphoreType.DMA((8,))],
        LAST_COST,
        base,
        rate,
        step,
        x_even,
        y_even,
        out_specs=(pltpu.HBM, VMEM),
    )
    peaks = lax.all_to_all(peak, AXES, 0, 0, tiled=True)
    (most,) = call(
        most_kernel, (SMEM((1,), jnp.float32),), [VMEM], [], 0, peaks, out_specs=(SMEM,)
    )
    return new, most.reshape(())


def solution(mesh):
    split = Mesh(mesh.devices.reshape(SIZES), AXES)
    spec = P(None, GX, GY, None)
    return jax.shard_map(
        local, mesh=split, in_specs=(spec, spec, P()), out_specs=(spec, P()), check_vma=False
    )
```

```python
import jax
import jax.numpy as jnp
from jax import lax
from jax.experimental import pallas as pl
from jax.experimental.pallas import tpu as pltpu
from jax.sharding import Mesh
from jax.sharding import PartitionSpec as P

GAMMA = 1.4
COURANT = 0.3
VISCOSITY = 0.05
CONDUCTION = 0.07
FIRST = (0.8, -0.2, 4.0 / 105.0, -1.0 / 280.0)
SECOND = (1.6, -0.2, 8.0 / 315.0, -1.0 / 560.0)
CENTRE = -205.0 / 72.0
AXES = ("z_lo", "y", "z_hi", "x", "core")
SIZES = (4, 8, 2, 4, 2)
GX, GY = AXES[:2], AXES[2:]
NEAR, FAR = ("y", "core"), ("z_lo", "z_hi", "x")
VMEM = pltpu.VMEM
SMEM = pltpu.SMEM
PACK_COST, INNER_COST, ODD_COST, EVEN_COST = 1 << 20, 1 << 20, 8 << 20, 1 << 20


def primitive(q):
    inverse = 1.0 / q[0]
    u, v, w = q[1] * inverse, q[2] * inverse, q[3] * inverse
    kinetic = 0.5 * (u * u + v * v + w * w)
    pressure = (GAMMA - 1.0) * (q[4] - q[0] * kinetic)
    return inverse, (u, v, w), kinetic, pressure


def flux(q, velocity, pressure, d):
    s = velocity[d]
    out = [q[1 + d], q[1] * s, q[2] * s, q[3] * s, (q[4] + pressure) * s]
    out[1 + d] = out[1 + d] + pressure
    return out


def smooth(inverse, velocity, kinetic, pressure):
    heat = VISCOSITY * kinetic + CONDUCTION * (pressure * inverse)
    return [None] + [VISCOSITY * s for s in velocity] + [heat]


def sides(f, g, m):
    first = FIRST[m - 1] * f
    if g is None:
        return -first, first
    second = SECOND[m - 1] * g
    return second - first, second + first


def odd(axis):
    return lax.rem(lax.axis_index(axis), 2)


def first_kernel(far_start, x_odd, sems):
    copies = [
        pltpu.make_async_copy(far_start.at[c, pl.ds(4 * odd("y"), 4)], x_odd.at[c], sems.at[c])
        for c in range(5)
    ]
    for copy in copies:
        copy.start()
    for copy in copies:
        copy.wait()


def pack_kernel(start, y_odd, x_even, y_even):
    side = odd("y")
    first = lax.broadcasted_iota(jnp.int32, (8, 256), 0) < 4
    upper = odd("core") == 0
    for c in range(5):
        x_even[c] = start[c, pl.ds(4 - 4 * side, 4)]
        for j in range(4):
            a, b = start[c, 2 * j, 0:8], start[c, 2 * j + 1, 0:8]
            low = jnp.where(first, a, pltpu.roll(b, 4, 0))
            a, b = start[c, 2 * j, 8:16], start[c, 2 * j + 1, 8:16]
            high = jnp.where(first, pltpu.roll(b, 4, 0), a)
            y_even[c, j] = jnp.where(upper, high, low)
            y_odd[c, j] = jnp.where(upper, low, high)


def inner_kernel(speed, start, section_far, out, step, section, fluxes, smooths, sems):
    copies = [
        pltpu.make_async_copy(section_far.at[:, i], section.at[:, i], sems.at[i]) for i in range(8)
    ]
    for copy in copies:
        copy.start()
    rows = lax.broadcasted_iota(jnp.int32, (16, 256), 0)

    def layer(i, carry):
        pltpu.make_async_copy(section_far.at[:, i], section.at[:, i], sems.at[i]).wait()
        q = [section[c, i] for c in range(5)]
        inverse, velocity, kinetic, pressure = primitive(q)
        g = smooth(inverse, velocity, kinetic, pressure)
        fx = flux(q, velocity, pressure, 0)
        fy = flux(q, velocity, pressure, 1)
        fz = flux(q, velocity, pressure, 2)
        for c in range(5):
            fluxes[c, i] = fx[c]
            total = jnp.zeros((16, 256), jnp.float32)
            if c:
                smooths[c - 1, i] = g[c]
                total = (3.0 * CENTRE) * g[c]
            for m in range(1, 5):
                up, down = sides(fz[c], g[c], m)
                total = total + pltpu.roll(up, 256 - m, 1) + pltpu.roll(down, m, 1)
                up, down = sides(fy[c], g[c], m)
                total = total + jnp.where(rows < 16 - m, pltpu.roll(up, 16 - m, 0), 0.0)
                total = total + jnp.where(rows >= m, pltpu.roll(down, m, 0), 0.0)
            out[c, i] = total
        return carry

    lax.fori_loop(0, 8, layer, 0)
    factor = (0.25 * COURANT) / jnp.broadcast_to(speed[...], (8, 128))
    step[...] = factor
    factor = jnp.tile(factor, (2, 2))
    for c in range(5):
        for i in range(8):
            total = out[c, i]
            for m in range(1, 5):
                for j, sign in ((i + m, -1.0), (i - m, 1.0)):
                    if 0 <= j < 8:
                        total = total + (sign * FIRST[m - 1]) * fluxes[c, j]
                        if c:
                            total = total + SECOND[m - 1] * smooths[c - 1, j]
            out[c, i] = 0.75 * start[c, i] + 0.25 * section[c, i] + factor * total


def y_side(rim, sums, below):
    rows = lax.broadcasted_iota(jnp.int32, (8, 256), 0)

    def pair(j, carry):
        q = [rim[c, j] for c in range(5)]
        inverse, velocity, kinetic, pressure = primitive(q)
        g = smooth(inverse, velocity, kinetic, pressure)
        f = flux(q, velocity, pressure, 1)
        for c in range(5):
            totals = [None, None]
            for m in range(1, 5):
                up, down = sides(f[c], g[c], m)
                for second in range(2):
                    if below:
                        part = jnp.where(rows < m, pltpu.roll(down, (m + 4 * second) % 8, 0), 0.0)
                    else:
                        part = jnp.where(rows >= 8 - m, pltpu.roll(up, (8 - m + 4 * second) % 8, 0), 0.0)
                    totals[second] = part if totals[second] is None else totals[second] + part
            sums[c, 2 * j] = totals[0]
            sums[c, 2 * j + 1] = totals[1]
        return carry

    lax.fori_loop(0, 4, pair, 0)


def rim_terms(x_below, y_below, x_rim, y_rim, fluxes, smooths, sums):
    @pl.when(y_below == 1)
    def _():
        y_side(y_rim, sums, True)

    @pl.when(y_below == 0)
    def _():
        y_side(y_rim, sums, False)

    sign = jnp.where(x_below == 1, 1.0, -1.0)

    def x_layer(d, carry):
        i = jnp.where(x_below == 1, 3 - d, d)
        q = [x_rim[c, i] for c in range(5)]
        inverse, velocity, kinetic, pressure = primitive(q)
        g = smooth(inverse, velocity, kinetic, pressure)
        f = flux(q, velocity, pressure, 0)
        for c in range(5):
            fluxes[c, d] = sign * f[c]
            if c:
                smooths[c - 1, d] = g[c]
        return carry

    lax.fori_loop(0, 4, x_layer, 0)


def rim_layer(t, x_below, y_below, inner, step, fluxes, smooths, sums):
    i = jnp.where(x_below == 1, t, 7 - t)
    factor = jnp.tile(step[...], (1, 2))
    low = jnp.where(y_below == 1, factor, 0.0)
    edge = jnp.concatenate([low, factor - low], axis=0)
    factor = jnp.concatenate([factor, factor], axis=0)
    values = []
    for c in range(5):
        part = sums[c, i]
        value = inner[c, i] + edge * jnp.concatenate([part, part], axis=0)
        total = None
        for d in range(4 - t):
            term = FIRST[d + t] * fluxes[c, d]
            if c:
                term = term + SECOND[d + t] * smooths[c - 1, d]
            total = term if total is None else total + term
        if total is not None:
            value = value + factor * total
        values.append(value)
    return i, values


def odd_kernel(inner, step, x_rim, y_rim, out, fluxes, smooths, sums):
    x_below, y_below = 1 - odd("y"), 1 - odd("core")
    rim_terms(x_below, y_below, x_rim, y_rim, fluxes, smooths, sums)
    for t in range(8):
        i, values = rim_layer(t, x_below, y_below, inner, step, fluxes, smooths, sums)
        for c in range(5):
            out[c, i] = values[c]


def even_kernel(inner, step, x_rim, y_rim, out, peak, fluxes, smooths, sums):
    x_below, y_below = odd("y"), odd("core")
    rim_terms(x_below, y_below, x_rim, y_rim, fluxes, smooths, sums)
    most = None
    for t in range(8):
        i, values = rim_layer(t, x_below, y_below, inner, step, fluxes, smooths, sums)
        for c in range(5):
            out[c, i] = values[c]
        inverse, velocity, kinetic, pressure = primitive(values)
        speed = jnp.sqrt(2.0 * kinetic) + jnp.sqrt(GAMMA * pressure * inverse)
        most = speed if most is None else jnp.maximum(most, speed)
    most = jnp.maximum(most[:, :128], most[:, 128:])
    spread(most, peak)


def spread(values, out):
    out[...] = jnp.broadcast_to(jnp.max(values, axis=0, keepdims=True), out.shape)


def pass_kernel(peaks, out):
    spread(peaks[...], out)


def most_kernel(peaks, out):
    out[0] = jnp.max(peaks[...])


def in_vmem(*sizes):
    return VMEM(sizes, jnp.float32)


def call(kernel, outs, in_specs, scratch, cost, *arrays, out_space=VMEM):
    estimate = pl.CostEstimate(flops=cost * 300, bytes_accessed=cost, transcendentals=0) if cost else None
    return pl.pallas_call(
        kernel,
        out_shape=outs,
        in_specs=[pl.BlockSpec(memory_space=m) for m in in_specs],
        out_specs=tuple(pl.BlockSpec(memory_space=out_space) for _ in outs),
        scratch_shapes=scratch,
        cost_estimate=estimate,
        compiler_params=pltpu.CompilerParams(vmem_limit_bytes=8 << 20),
    )(*arrays)


def far(x):
    return pltpu.with_memory_space_constraint(x, pltpu.HBM)


def swap(x, axis, offset):
    n = lax.axis_size(axis)
    pairs = [((i + offset) % n, (i + 1 + offset) % n) for i in range(0, n, 2)]
    return lax.ppermute(x, axis, pairs + [(b, a) for a, b in pairs])


def local(start, section, previous_speed):
    x_rim, y_rim = in_vmem(5, 4, 16, 256), in_vmem(5, 4, 8, 256)
    (x_odd,) = call(
        first_kernel, (x_rim,), [pltpu.HBM], [pltpu.SemaphoreType.DMA((5,))], 0, far(start)
    )
    y_odd, x_even, y_even = call(pack_kernel, (y_rim, x_rim, y_rim), [VMEM], [], PACK_COST, start)
    x_odd, y_odd = swap(x_odd, GX, 1), swap(y_odd, GY, 1)
    y_even, x_even = swap(y_even, GY, 0), swap(x_even, GX, 0)
    state = in_vmem(5, 8, 16, 256)
    inner, step = call(
        inner_kernel,
        (state, in_vmem(8, 128)),
        [VMEM, VMEM, pltpu.HBM],
        [
            state,
            state,
            in_vmem(4, 8, 16, 256),
            pltpu.SemaphoreType.DMA((8,)),
        ],
        INNER_COST,
        previous_speed.reshape(1, 1),
        start,
        far(section),
    )
    rims = [in_vmem(5, 4, 16, 256), in_vmem(4, 4, 16, 256), in_vmem(5, 8, 8, 256)]
    (inner,) = call(odd_kernel, (state,), [VMEM] * 4, rims, ODD_COST, inner, step, x_odd, y_odd)
    new, peak = call(
        even_kernel,
        (state, in_vmem(lax.axis_size(NEAR), 128)),
        [VMEM] * 4,
        rims,
        EVEN_COST,
        inner,
        step,
        x_even,
        y_even,
    )
    peaks = lax.all_to_all(peak, NEAR, 0, 0, tiled=True)
    (peak,) = call(pass_kernel, (in_vmem(lax.axis_size(FAR), 128),), [VMEM], [], 0, peaks)
    peaks = lax.all_to_all(peak, FAR, 0, 0, tiled=True)
    (most,) = call(
        most_kernel, (SMEM((1,), jnp.float32),), [VMEM], [], 0, peaks, out_space=SMEM
    )
    return new, most.reshape(())


def solution(mesh):
    split = Mesh(mesh.devices.reshape(SIZES), AXES)
    spec = P(None, GX, GY, None)
    return jax.shard_map(
        local, mesh=split, in_specs=(spec, spec, P()), out_specs=(spec, P()), check_vma=False
    )
```

```python
import jax
import jax.numpy as jnp
from jax import lax
from jax.experimental import pallas as pl
from jax.experimental.pallas import tpu as pltpu
from jax.sharding import Mesh
from jax.sharding import PartitionSpec as P

GAMMA = 1.4
COURANT = 0.3
VISCOSITY = 0.05
CONDUCTION = 0.07
FIRST = (0.8, -0.2, 4.0 / 105.0, -1.0 / 280.0)
SECOND = (1.6, -0.2, 8.0 / 315.0, -1.0 / 560.0)
CENTRE = -205.0 / 72.0
AXES = ("z_lo", "y", "z_hi", "x", "core")
SIZES = (4, 8, 2, 4, 2)
GX, GY = AXES[:2], AXES[2:]
NEAR, FAR = ("y", "core"), ("z_lo", "z_hi", "x")
VMEM = pltpu.VMEM
SMEM = pltpu.SMEM
PACK_COST, INNER_COST, ODD_COST, EVEN_COST = 1 << 20, 1 << 20, 7 << 20, 1 << 19


def primitive(q):
    inverse = 1.0 / q[0]
    u, v, w = q[1] * inverse, q[2] * inverse, q[3] * inverse
    kinetic = 0.5 * (u * u + v * v + w * w)
    pressure = (GAMMA - 1.0) * (q[4] - q[0] * kinetic)
    return inverse, (u, v, w), kinetic, pressure


def flux(q, velocity, pressure, d):
    s = velocity[d]
    out = [q[1 + d], q[1] * s, q[2] * s, q[3] * s, (q[4] + pressure) * s]
    out[1 + d] = out[1 + d] + pressure
    return out


def smooth(inverse, velocity, kinetic, pressure):
    heat = VISCOSITY * kinetic + CONDUCTION * (pressure * inverse)
    return [None] + [VISCOSITY * s for s in velocity] + [heat]


def sides(f, g, m):
    first = FIRST[m - 1] * f
    if g is None:
        return -first, first
    second = SECOND[m - 1] * g
    return second - first, second + first


def odd(axis):
    return lax.rem(lax.axis_index(axis), 2)


def first_kernel(far_start, x_odd, sems):
    copies = [
        pltpu.make_async_copy(far_start.at[c, pl.ds(4 * odd("y"), 4)], x_odd.at[c], sems.at[c])
        for c in range(5)
    ]
    for copy in copies:
        copy.start()
    for copy in copies:
        copy.wait()


def pack_kernel(start, y_odd, x_even, y_even):
    side = odd("y")
    first = lax.broadcasted_iota(jnp.int32, (8, 256), 0) < 4
    upper = odd("core") == 0
    for c in range(5):
        x_even[c] = start[c, pl.ds(4 - 4 * side, 4)]
        for j in range(4):
            a, b = start[c, 2 * j, 0:8], start[c, 2 * j + 1, 0:8]
            low = jnp.where(first, a, pltpu.roll(b, 4, 0))
            a, b = start[c, 2 * j, 8:16], start[c, 2 * j + 1, 8:16]
            high = jnp.where(first, pltpu.roll(b, 4, 0), a)
            y_even[c, j] = jnp.where(upper, high, low)
            y_odd[c, j] = jnp.where(upper, low, high)


def inner_kernel(speed, start, section_far, out, step, section, fluxes, smooths, sems):
    def load(i):
        return pltpu.make_async_copy(section_far.at[:, i], section.at[:, i], sems.at[i])

    load(0).start()
    load(1).start()
    rows = lax.broadcasted_iota(jnp.int32, (16, 256), 0)

    def layer(i, carry):
        load(i).wait()

        @pl.when(i < 6)
        def _():
            load(i + 2).start()

        q = [section[c, i] for c in range(5)]
        inverse, velocity, kinetic, pressure = primitive(q)
        g = smooth(inverse, velocity, kinetic, pressure)
        fx = flux(q, velocity, pressure, 0)
        fy = flux(q, velocity, pressure, 1)
        fz = flux(q, velocity, pressure, 2)
        for c in range(5):
            fluxes[c, i] = fx[c]
            total = jnp.zeros((16, 256), jnp.float32)
            if c:
                smooths[c - 1, i] = g[c]
                total = (3.0 * CENTRE) * g[c]
            for m in range(1, 5):
                up, down = sides(fz[c], g[c], m)
                total = total + pltpu.roll(up, 256 - m, 1) + pltpu.roll(down, m, 1)
                up, down = sides(fy[c], g[c], m)
                total = total + jnp.where(rows < 16 - m, pltpu.roll(up, 16 - m, 0), 0.0)
                total = total + jnp.where(rows >= m, pltpu.roll(down, m, 0), 0.0)
            out[c, i] = total
        return carry

    lax.fori_loop(0, 8, layer, 0)
    factor = (0.25 * COURANT) / jnp.broadcast_to(speed[...], (8, 128))
    step[...] = factor
    factor = jnp.tile(factor, (2, 2))
    for c in range(5):
        for i in range(8):
            total = out[c, i]
            for m in range(1, 5):
                for j, sign in ((i + m, -1.0), (i - m, 1.0)):
                    if 0 <= j < 8:
                        total = total + (sign * FIRST[m - 1]) * fluxes[c, j]
                        if c:
                            total = total + SECOND[m - 1] * smooths[c - 1, j]
            out[c, i] = 0.75 * start[c, i] + 0.25 * section[c, i] + factor * total


def y_side(rim, sums, below):
    rows = lax.broadcasted_iota(jnp.int32, (8, 256), 0)

    def pair(j, carry):
        q = [rim[c, j] for c in range(5)]
        inverse, velocity, kinetic, pressure = primitive(q)
        g = smooth(inverse, velocity, kinetic, pressure)
        f = flux(q, velocity, pressure, 1)
        for c in range(5):
            totals = [None, None]
            for m in range(1, 5):
                up, down = sides(f[c], g[c], m)
                for second in range(2):
                    if below:
                        part = jnp.where(rows < m, pltpu.roll(down, (m + 4 * second) % 8, 0), 0.0)
                    else:
                        part = jnp.where(rows >= 8 - m, pltpu.roll(up, (8 - m + 4 * second) % 8, 0), 0.0)
                    totals[second] = part if totals[second] is None else totals[second] + part
            sums[c, 2 * j] = totals[0]
            sums[c, 2 * j + 1] = totals[1]
        return carry

    lax.fori_loop(0, 4, pair, 0)


def y_terms(y_below, y_rim, sums):
    @pl.when(y_below == 1)
    def _():
        y_side(y_rim, sums, True)

    @pl.when(y_below == 0)
    def _():
        y_side(y_rim, sums, False)


def x_terms(x_below, x_rim, fluxes, smooths):
    sign = jnp.where(x_below == 1, 1.0, -1.0)

    def x_layer(d, carry):
        i = jnp.where(x_below == 1, 3 - d, d)
        q = [x_rim[c, i] for c in range(5)]
        inverse, velocity, kinetic, pressure = primitive(q)
        g = smooth(inverse, velocity, kinetic, pressure)
        f = flux(q, velocity, pressure, 0)
        for c in range(5):
            fluxes[c, d] = sign * f[c]
            if c:
                smooths[c - 1, d] = g[c]
        return carry

    lax.fori_loop(0, 4, x_layer, 0)


def rim_layer(t, x_below, y_below, inner, step, fluxes, smooths, sums):
    i = jnp.where(x_below == 1, t, 7 - t)
    factor = jnp.tile(step[...], (1, 2))
    if sums is not None:
        low = jnp.where(y_below == 1, factor, 0.0)
        edge = jnp.concatenate([low, factor - low], axis=0)
    factor = jnp.concatenate([factor, factor], axis=0)
    values = []
    for c in range(5):
        value = inner[c, i]
        if sums is not None:
            part = sums[c, i]
            value = value + edge * jnp.concatenate([part, part], axis=0)
        total = None
        for d in range(4 - t) if fluxes is not None else ():
            term = FIRST[d + t] * fluxes[c, d]
            if c:
                term = term + SECOND[d + t] * smooths[c - 1, d]
            total = term if total is None else total + term
        if total is not None:
            value = value + factor * total
        values.append(value)
    return i, values


def odd_kernel(inner, step, x_rim, y_rim, out, fluxes, smooths, sums):
    x_below, y_below = 1 - odd("y"), 1 - odd("core")
    y_terms(y_below, y_rim, sums)
    x_terms(x_below, x_rim, fluxes, smooths)
    for t in range(8):
        i, values = rim_layer(t, x_below, y_below, inner, step, fluxes, smooths, sums)
        for c in range(5):
            out[c, i] = values[c]


def y_kernel(inner, step, y_rim, out, sums):
    y_below = odd("core")
    y_terms(y_below, y_rim, sums)
    for t in range(8):
        i, values = rim_layer(t, 1, y_below, inner, step, None, None, sums)
        for c in range(5):
            out[c, i] = values[c]


def even_kernel(inner, step, x_rim, out, peak, fluxes, smooths):
    x_below = odd("y")
    x_terms(x_below, x_rim, fluxes, smooths)
    most = None
    for t in range(8):
        i, values = rim_layer(t, x_below, None, inner, step, fluxes, smooths, None)
        for c in range(5):
            out[c, i] = values[c]
        inverse, velocity, kinetic, pressure = primitive(values)
        speed = jnp.sqrt(2.0 * kinetic) + jnp.sqrt(GAMMA * pressure * inverse)
        most = speed if most is None else jnp.maximum(most, speed)
    most = jnp.maximum(most[:, :128], most[:, 128:])
    spread(most, peak)


def spread(values, out):
    out[...] = jnp.broadcast_to(jnp.max(values, axis=0, keepdims=True), out.shape)


def pass_kernel(peaks, out):
    spread(peaks[...], out)


def most_kernel(peaks, out):
    out[0] = jnp.max(peaks[...])


def in_vmem(*sizes):
    return VMEM(sizes, jnp.float32)


def call(kernel, outs, in_specs, scratch, cost, *arrays, out_space=VMEM):
    estimate = pl.CostEstimate(flops=cost * 300, bytes_accessed=cost, transcendentals=0) if cost else None
    return pl.pallas_call(
        kernel,
        out_shape=outs,
        in_specs=[pl.BlockSpec(memory_space=m) for m in in_specs],
        out_specs=tuple(pl.BlockSpec(memory_space=out_space) for _ in outs),
        scratch_shapes=scratch,
        cost_estimate=estimate,
        compiler_params=pltpu.CompilerParams(vmem_limit_bytes=8 << 20),
    )(*arrays)


def far(x):
    return pltpu.with_memory_space_constraint(x, pltpu.HBM)


def swap(x, axis, offset):
    n = lax.axis_size(axis)
    pairs = [((i + offset) % n, (i + 1 + offset) % n) for i in range(0, n, 2)]
    return lax.ppermute(x, axis, pairs + [(b, a) for a, b in pairs])


def local(start, section, previous_speed):
    x_rim, y_rim = in_vmem(5, 4, 16, 256), in_vmem(5, 4, 8, 256)
    (x_odd,) = call(
        first_kernel, (x_rim,), [pltpu.HBM], [pltpu.SemaphoreType.DMA((5,))], 0, far(start)
    )
    y_odd, x_even, y_even = call(pack_kernel, (y_rim, x_rim, y_rim), [VMEM], [], PACK_COST, start)
    x_odd, y_odd = swap(x_odd, GX, 1), swap(y_odd, GY, 1)
    y_even, x_even = swap(y_even, GY, 0), swap(x_even, GX, 0)
    state = in_vmem(5, 8, 16, 256)
    inner, step = call(
        inner_kernel,
        (state, in_vmem(8, 128)),
        [VMEM, VMEM, pltpu.HBM],
        [
            state,
            state,
            in_vmem(4, 8, 16, 256),
            pltpu.SemaphoreType.DMA((8,)),
        ],
        INNER_COST,
        previous_speed.reshape(1, 1),
        start,
        far(section),
    )
    rims, sums = [x_rim, in_vmem(4, 4, 16, 256)], in_vmem(5, 8, 8, 256)
    (inner,) = call(
        odd_kernel, (state,), [VMEM] * 4, rims + [sums], ODD_COST, inner, step, x_odd, y_odd
    )
    (inner,) = call(y_kernel, (state,), [VMEM] * 3, [sums], EVEN_COST, inner, step, y_even)
    new, peak = call(
        even_kernel,
        (state, in_vmem(lax.axis_size(NEAR), 128)),
        [VMEM] * 3,
        rims,
        EVEN_COST,
        inner,
        step,
        x_even,
    )
    peaks = lax.all_to_all(peak, NEAR, 0, 0, tiled=True)
    (peak,) = call(pass_kernel, (in_vmem(lax.axis_size(FAR), 128),), [VMEM], [], 0, peaks)
    peaks = lax.all_to_all(peak, FAR, 0, 0, tiled=True)
    (most,) = call(
        most_kernel, (SMEM((1,), jnp.float32),), [VMEM], [], 0, peaks, out_space=SMEM
    )
    return new, most.reshape(())


def solution(mesh):
    split = Mesh(mesh.devices.reshape(SIZES), AXES)
    spec = P(None, GX, GY, None)
    return jax.shard_map(
        local, mesh=split, in_specs=(spec, spec, P()), out_specs=(spec, P()), check_vma=False
    )
```

```python
import jax
import jax.numpy as jnp
from jax import lax
from jax.experimental import pallas as pl
from jax.experimental.pallas import tpu as pltpu
from jax.sharding import Mesh
from jax.sharding import PartitionSpec as P

GAMMA = 1.4
COURANT = 0.3
VISCOSITY = 0.05
CONDUCTION = 0.07
FIRST = (0.8, -0.2, 4.0 / 105.0, -1.0 / 280.0)
SECOND = (1.6, -0.2, 8.0 / 315.0, -1.0 / 560.0)
CENTRE = -205.0 / 72.0
AXES = ("z_lo", "y", "z_hi", "x", "core")
SIZES = (4, 8, 2, 4, 2)
GX, GY = AXES[:2], AXES[2:]
NEAR, FAR = ("y", "core"), ("z_lo", "z_hi", "x")
VMEM = pltpu.VMEM
SMEM = pltpu.SMEM
PACK_COST, INNER_COST, ODD_COST, EVEN_COST = 1 << 20, 1 << 20, 7 << 20, 1 << 19


def primitive(q):
    inverse = 1.0 / q[0]
    u, v, w = q[1] * inverse, q[2] * inverse, q[3] * inverse
    kinetic = 0.5 * (u * u + v * v + w * w)
    pressure = (GAMMA - 1.0) * (q[4] - q[0] * kinetic)
    return inverse, (u, v, w), kinetic, pressure


def flux(q, velocity, pressure, d):
    s = velocity[d]
    out = [q[1 + d], q[1] * s, q[2] * s, q[3] * s, (q[4] + pressure) * s]
    out[1 + d] = out[1 + d] + pressure
    return out


def smooth(inverse, velocity, kinetic, pressure):
    heat = VISCOSITY * kinetic + CONDUCTION * (pressure * inverse)
    return [None] + [VISCOSITY * s for s in velocity] + [heat]


def sides(f, g, m):
    first = FIRST[m - 1] * f
    if g is None:
        return -first, first
    second = SECOND[m - 1] * g
    return second - first, second + first


def odd(axis):
    return lax.rem(lax.axis_index(axis), 2)


def first_kernel(far_start, x_odd, sems):
    copies = [
        pltpu.make_async_copy(far_start.at[c, pl.ds(4 * odd("y"), 4)], x_odd.at[c], sems.at[c])
        for c in range(5)
    ]
    for copy in copies:
        copy.start()
    for copy in copies:
        copy.wait()


def pack_kernel(start, y_odd, x_even, y_even):
    side = odd("y")
    first = lax.broadcasted_iota(jnp.int32, (8, 256), 0) < 4
    upper = odd("core") == 0
    for c in range(5):
        x_even[c] = start[c, pl.ds(4 - 4 * side, 4)]
        for j in range(4):
            a, b = start[c, 2 * j, 0:8], start[c, 2 * j + 1, 0:8]
            low = jnp.where(first, a, pltpu.roll(b, 4, 0))
            a, b = start[c, 2 * j, 8:16], start[c, 2 * j + 1, 8:16]
            high = jnp.where(first, pltpu.roll(b, 4, 0), a)
            y_even[c, j] = jnp.where(upper, high, low)
            y_odd[c, j] = jnp.where(upper, low, high)


def inner_kernel(speed, start, section_far, out, step, section, fluxes, smooths, sems):
    def loads(half):
        rows = pl.ds(4 * half, 4)
        return [
            pltpu.make_async_copy(section_far.at[c, rows], section.at[c, rows], sems.at[half, c])
            for c in range(5)
        ]

    for half in range(2):
        for copy in loads(half):
            copy.start()
    rows = lax.broadcasted_iota(jnp.int32, (16, 256), 0)

    def layer(i, carry):
        for half in range(2):

            @pl.when(i == 4 * half)
            def _(half=half):
                for copy in loads(half):
                    copy.wait()

        q = [section[c, i] for c in range(5)]
        inverse, velocity, kinetic, pressure = primitive(q)
        g = smooth(inverse, velocity, kinetic, pressure)
        fx = flux(q, velocity, pressure, 0)
        fy = flux(q, velocity, pressure, 1)
        fz = flux(q, velocity, pressure, 2)
        for c in range(5):
            fluxes[c, i] = fx[c]
            total = jnp.zeros((16, 256), jnp.float32)
            if c:
                smooths[c - 1, i] = g[c]
                total = (3.0 * CENTRE) * g[c]
            for m in range(1, 5):
                up, down = sides(fz[c], g[c], m)
                total = total + pltpu.roll(up, 256 - m, 1) + pltpu.roll(down, m, 1)
                up, down = sides(fy[c], g[c], m)
                total = total + jnp.where(rows < 16 - m, pltpu.roll(up, 16 - m, 0), 0.0)
                total = total + jnp.where(rows >= m, pltpu.roll(down, m, 0), 0.0)
            out[c, i] = total
        return carry

    lax.fori_loop(0, 8, layer, 0)
    factor = (0.25 * COURANT) / jnp.broadcast_to(speed[...], (8, 128))
    step[...] = factor
    factor = jnp.tile(factor, (2, 2))
    for c in range(5):
        for i in range(8):
            total = out[c, i]
            for m in range(1, 5):
                for j, sign in ((i + m, -1.0), (i - m, 1.0)):
                    if 0 <= j < 8:
                        total = total + (sign * FIRST[m - 1]) * fluxes[c, j]
                        if c:
                            total = total + SECOND[m - 1] * smooths[c - 1, j]
            out[c, i] = 0.75 * start[c, i] + 0.25 * section[c, i] + factor * total


def y_side(rim, sums, below):
    rows = lax.broadcasted_iota(jnp.int32, (8, 256), 0)

    def pair(j, carry):
        q = [rim[c, j] for c in range(5)]
        inverse, velocity, kinetic, pressure = primitive(q)
        g = smooth(inverse, velocity, kinetic, pressure)
        f = flux(q, velocity, pressure, 1)
        for c in range(5):
            totals = [None, None]
            for m in range(1, 5):
                up, down = sides(f[c], g[c], m)
                for second in range(2):
                    if below:
                        part = jnp.where(rows < m, pltpu.roll(down, (m + 4 * second) % 8, 0), 0.0)
                    else:
                        part = jnp.where(rows >= 8 - m, pltpu.roll(up, (8 - m + 4 * second) % 8, 0), 0.0)
                    totals[second] = part if totals[second] is None else totals[second] + part
            sums[c, 2 * j] = totals[0]
            sums[c, 2 * j + 1] = totals[1]
        return carry

    lax.fori_loop(0, 4, pair, 0)


def y_terms(y_below, y_rim, sums):
    @pl.when(y_below == 1)
    def _():
        y_side(y_rim, sums, True)

    @pl.when(y_below == 0)
    def _():
        y_side(y_rim, sums, False)


def x_terms(x_below, x_rim, fluxes, smooths):
    sign = jnp.where(x_below == 1, 1.0, -1.0)

    def x_layer(d, carry):
        i = jnp.where(x_below == 1, 3 - d, d)
        q = [x_rim[c, i] for c in range(5)]
        inverse, velocity, kinetic, pressure = primitive(q)
        g = smooth(inverse, velocity, kinetic, pressure)
        f = flux(q, velocity, pressure, 0)
        for c in range(5):
            fluxes[c, d] = sign * f[c]
            if c:
                smooths[c - 1, d] = g[c]
        return carry

    lax.fori_loop(0, 4, x_layer, 0)


def rim_layer(t, x_below, y_below, inner, step, fluxes, smooths, sums):
    i = jnp.where(x_below == 1, t, 7 - t)
    factor = jnp.tile(step[...], (1, 2))
    if sums is not None:
        low = jnp.where(y_below == 1, factor, 0.0)
        edge = jnp.concatenate([low, factor - low], axis=0)
    factor = jnp.concatenate([factor, factor], axis=0)
    values = []
    for c in range(5):
        value = inner[c, i]
        if sums is not None:
            part = sums[c, i]
            value = value + edge * jnp.concatenate([part, part], axis=0)
        total = None
        for d in range(4 - t) if fluxes is not None else ():
            term = FIRST[d + t] * fluxes[c, d]
            if c:
                term = term + SECOND[d + t] * smooths[c - 1, d]
            total = term if total is None else total + term
        if total is not None:
            value = value + factor * total
        values.append(value)
    return i, values


def odd_kernel(inner, step, x_rim, y_rim, out, fluxes, smooths, sums):
    x_below, y_below = 1 - odd("y"), 1 - odd("core")
    y_terms(y_below, y_rim, sums)
    x_terms(x_below, x_rim, fluxes, smooths)
    for t in range(8):
        i, values = rim_layer(t, x_below, y_below, inner, step, fluxes, smooths, sums)
        for c in range(5):
            out[c, i] = values[c]


def y_kernel(inner, step, y_rim, out, sums):
    y_below = odd("core")
    y_terms(y_below, y_rim, sums)
    for t in range(8):
        i, values = rim_layer(t, 1, y_below, inner, step, None, None, sums)
        for c in range(5):
            out[c, i] = values[c]


def even_kernel(inner, step, x_rim, out, peak, fluxes, smooths):
    x_below = odd("y")
    x_terms(x_below, x_rim, fluxes, smooths)
    most = None
    for t in range(8):
        i, values = rim_layer(t, x_below, None, inner, step, fluxes, smooths, None)
        for c in range(5):
            out[c, i] = values[c]
        inverse, velocity, kinetic, pressure = primitive(values)
        speed = jnp.sqrt(2.0 * kinetic) + jnp.sqrt(GAMMA * pressure * inverse)
        most = speed if most is None else jnp.maximum(most, speed)
    most = jnp.maximum(most[:, :128], most[:, 128:])
    spread(most, peak)


def spread(values, out):
    out[...] = jnp.broadcast_to(jnp.max(values, axis=0, keepdims=True), out.shape)


def pass_kernel(peaks, out):
    spread(peaks[...], out)


def most_kernel(peaks, out):
    out[0] = jnp.max(peaks[...])


def in_vmem(*sizes):
    return VMEM(sizes, jnp.float32)


def call(kernel, outs, in_specs, scratch, cost, *arrays, out_space=VMEM):
    estimate = pl.CostEstimate(flops=cost * 300, bytes_accessed=cost, transcendentals=0) if cost else None
    return pl.pallas_call(
        kernel,
        out_shape=outs,
        in_specs=[pl.BlockSpec(memory_space=m) for m in in_specs],
        out_specs=tuple(pl.BlockSpec(memory_space=out_space) for _ in outs),
        scratch_shapes=scratch,
        cost_estimate=estimate,
        compiler_params=pltpu.CompilerParams(vmem_limit_bytes=8 << 20),
    )(*arrays)


def far(x):
    return pltpu.with_memory_space_constraint(x, pltpu.HBM)


def swap(x, axis, offset):
    n = lax.axis_size(axis)
    pairs = [((i + offset) % n, (i + 1 + offset) % n) for i in range(0, n, 2)]
    return lax.ppermute(x, axis, pairs + [(b, a) for a, b in pairs])


def local(start, section, previous_speed):
    x_rim, y_rim = in_vmem(5, 4, 16, 256), in_vmem(5, 4, 8, 256)
    (x_odd,) = call(
        first_kernel, (x_rim,), [pltpu.HBM], [pltpu.SemaphoreType.DMA((5,))], 0, far(start)
    )
    y_odd, x_even, y_even = call(pack_kernel, (y_rim, x_rim, y_rim), [VMEM], [], PACK_COST, start)
    x_odd, y_odd = swap(x_odd, GX, 1), swap(y_odd, GY, 1)
    y_even, x_even = swap(y_even, GY, 0), swap(x_even, GX, 0)
    state = in_vmem(5, 8, 16, 256)
    inner, step = call(
        inner_kernel,
        (state, in_vmem(8, 128)),
        [VMEM, VMEM, pltpu.HBM],
        [
            state,
            state,
            in_vmem(4, 8, 16, 256),
            pltpu.SemaphoreType.DMA((2, 5)),
        ],
        INNER_COST,
        previous_speed.reshape(1, 1),
        start,
        far(section),
    )
    rims, sums = [x_rim, in_vmem(4, 4, 16, 256)], in_vmem(5, 8, 8, 256)
    (inner,) = call(
        odd_kernel, (state,), [VMEM] * 4, rims + [sums], ODD_COST, inner, step, x_odd, y_odd
    )
    (inner,) = call(y_kernel, (state,), [VMEM] * 3, [sums], EVEN_COST, inner, step, y_even)
    new, peak = call(
        even_kernel,
        (state, in_vmem(lax.axis_size(NEAR), 128)),
        [VMEM] * 3,
        rims,
        EVEN_COST,
        inner,
        step,
        x_even,
    )
    peaks = lax.all_to_all(peak, NEAR, 0, 0, tiled=True)
    (peak,) = call(pass_kernel, (in_vmem(lax.axis_size(FAR), 128),), [VMEM], [], 0, peaks)
    peaks = lax.all_to_all(peak, FAR, 0, 0, tiled=True)
    (most,) = call(
        most_kernel, (SMEM((1,), jnp.float32),), [VMEM], [], 0, peaks, out_space=SMEM
    )
    return new, most.reshape(())


def solution(mesh):
    split = Mesh(mesh.devices.reshape(SIZES), AXES)
    spec = P(None, GX, GY, None)
    return jax.shard_map(
        local, mesh=split, in_specs=(spec, spec, P()), out_specs=(spec, P()), check_vma=False
    )
```

```python
import jax
import jax.numpy as jnp
from jax import lax
from jax.experimental import pallas as pl
from jax.experimental.pallas import tpu as pltpu
from jax.sharding import Mesh
from jax.sharding import PartitionSpec as P

GAMMA = 1.4
COURANT = 0.3
VISCOSITY = 0.05
CONDUCTION = 0.07
FIRST = (0.8, -0.2, 4.0 / 105.0, -1.0 / 280.0)
SECOND = (1.6, -0.2, 8.0 / 315.0, -1.0 / 560.0)
CENTRE = -205.0 / 72.0
AXES = ("z_lo", "y", "z_hi", "x", "core")
SIZES = (4, 8, 2, 4, 2)
GX, GY = AXES[:2], AXES[2:]
NEAR, FAR = ("y", "x", "core"), ("z_lo", "z_hi")
VMEM = pltpu.VMEM
SMEM = pltpu.SMEM
PACK_COST, INNER_COST, ODD_COST, EVEN_COST = 1 << 20, 1 << 20, 7 << 20, 1 << 19


def primitive(q):
    inverse = 1.0 / q[0]
    u, v, w = q[1] * inverse, q[2] * inverse, q[3] * inverse
    kinetic = 0.5 * (u * u + v * v + w * w)
    pressure = (GAMMA - 1.0) * (q[4] - q[0] * kinetic)
    return inverse, (u, v, w), kinetic, pressure


def flux(q, velocity, pressure, d):
    s = velocity[d]
    out = [q[1 + d], q[1] * s, q[2] * s, q[3] * s, (q[4] + pressure) * s]
    out[1 + d] = out[1 + d] + pressure
    return out


def smooth(inverse, velocity, kinetic, pressure):
    heat = VISCOSITY * kinetic + CONDUCTION * (pressure * inverse)
    return [None] + [VISCOSITY * s for s in velocity] + [heat]


def sides(f, g, m):
    first = FIRST[m - 1] * f
    if g is None:
        return -first, first
    second = SECOND[m - 1] * g
    return second - first, second + first


def odd(axis):
    return lax.rem(lax.axis_index(axis), 2)


def first_kernel(far_start, x_odd, sems):
    copies = [
        pltpu.make_async_copy(far_start.at[c, pl.ds(4 * odd("y"), 4)], x_odd.at[c], sems.at[c])
        for c in range(5)
    ]
    for copy in copies:
        copy.start()
    for copy in copies:
        copy.wait()


def pack_kernel(start, y_odd, x_even, y_even):
    side = odd("y")
    first = lax.broadcasted_iota(jnp.int32, (8, 256), 0) < 4
    upper = odd("core") == 0
    for c in range(5):
        x_even[c] = start[c, pl.ds(4 - 4 * side, 4)]
        for j in range(4):
            a, b = start[c, 2 * j, 0:8], start[c, 2 * j + 1, 0:8]
            low = jnp.where(first, a, pltpu.roll(b, 4, 0))
            a, b = start[c, 2 * j, 8:16], start[c, 2 * j + 1, 8:16]
            high = jnp.where(first, pltpu.roll(b, 4, 0), a)
            y_even[c, j] = jnp.where(upper, high, low)
            y_odd[c, j] = jnp.where(upper, low, high)


def inner_kernel(speed, start, section_far, out, step, section, fluxes, smooths, sems):
    def loads(half):
        rows = pl.ds(4 * half, 4)
        return [
            pltpu.make_async_copy(section_far.at[c, rows], section.at[c, rows], sems.at[half, c])
            for c in range(5)
        ]

    for half in range(2):
        for copy in loads(half):
            copy.start()
    rows = lax.broadcasted_iota(jnp.int32, (16, 256), 0)

    def layer(i, carry):
        for half in range(2):

            @pl.when(i == 4 * half)
            def _(half=half):
                for copy in loads(half):
                    copy.wait()

        q = [section[c, i] for c in range(5)]
        inverse, velocity, kinetic, pressure = primitive(q)
        g = smooth(inverse, velocity, kinetic, pressure)
        fx = flux(q, velocity, pressure, 0)
        fy = flux(q, velocity, pressure, 1)
        fz = flux(q, velocity, pressure, 2)
        for c in range(5):
            fluxes[c, i] = fx[c]
            total = jnp.zeros((16, 256), jnp.float32)
            if c:
                smooths[c - 1, i] = g[c]
                total = (3.0 * CENTRE) * g[c]
            for m in range(1, 5):
                up, down = sides(fz[c], g[c], m)
                total = total + pltpu.roll(up, 256 - m, 1) + pltpu.roll(down, m, 1)
                up, down = sides(fy[c], g[c], m)
                total = total + jnp.where(rows < 16 - m, pltpu.roll(up, 16 - m, 0), 0.0)
                total = total + jnp.where(rows >= m, pltpu.roll(down, m, 0), 0.0)
            out[c, i] = total
        return carry

    lax.fori_loop(0, 8, layer, 0)
    factor = (0.25 * COURANT) / jnp.broadcast_to(speed[...], (8, 128))
    step[...] = factor
    factor = jnp.tile(factor, (2, 2))
    for c in range(5):
        for i in range(8):
            total = out[c, i]
            for m in range(1, 5):
                for j, sign in ((i + m, -1.0), (i - m, 1.0)):
                    if 0 <= j < 8:
                        total = total + (sign * FIRST[m - 1]) * fluxes[c, j]
                        if c:
                            total = total + SECOND[m - 1] * smooths[c - 1, j]
            out[c, i] = 0.75 * start[c, i] + 0.25 * section[c, i] + factor * total


def y_side(rim, sums, below):
    rows = lax.broadcasted_iota(jnp.int32, (8, 256), 0)

    def pair(j, carry):
        q = [rim[c, j] for c in range(5)]
        inverse, velocity, kinetic, pressure = primitive(q)
        g = smooth(inverse, velocity, kinetic, pressure)
        f = flux(q, velocity, pressure, 1)
        for c in range(5):
            totals = [None, None]
            for m in range(1, 5):
                up, down = sides(f[c], g[c], m)
                for second in range(2):
                    if below:
                        part = jnp.where(rows < m, pltpu.roll(down, (m + 4 * second) % 8, 0), 0.0)
                    else:
                        part = jnp.where(rows >= 8 - m, pltpu.roll(up, (8 - m + 4 * second) % 8, 0), 0.0)
                    totals[second] = part if totals[second] is None else totals[second] + part
            sums[c, 2 * j] = totals[0]
            sums[c, 2 * j + 1] = totals[1]
        return carry

    lax.fori_loop(0, 4, pair, 0)


def y_terms(y_below, y_rim, sums):
    @pl.when(y_below == 1)
    def _():
        y_side(y_rim, sums, True)

    @pl.when(y_below == 0)
    def _():
        y_side(y_rim, sums, False)


def x_terms(x_below, x_rim, fluxes, smooths):
    sign = jnp.where(x_below == 1, 1.0, -1.0)

    def x_layer(d, carry):
        i = jnp.where(x_below == 1, 3 - d, d)
        q = [x_rim[c, i] for c in range(5)]
        inverse, velocity, kinetic, pressure = primitive(q)
        g = smooth(inverse, velocity, kinetic, pressure)
        f = flux(q, velocity, pressure, 0)
        for c in range(5):
            fluxes[c, d] = sign * f[c]
            if c:
                smooths[c - 1, d] = g[c]
        return carry

    lax.fori_loop(0, 4, x_layer, 0)


def rim_layer(t, x_below, y_below, inner, step, fluxes, smooths, sums):
    i = jnp.where(x_below == 1, t, 7 - t)
    factor = jnp.tile(step[...], (1, 2))
    if sums is not None:
        low = jnp.where(y_below == 1, factor, 0.0)
        edge = jnp.concatenate([low, factor - low], axis=0)
    factor = jnp.concatenate([factor, factor], axis=0)
    values = []
    for c in range(5):
        value = inner[c, i]
        if sums is not None:
            part = sums[c, i]
            value = value + edge * jnp.concatenate([part, part], axis=0)
        total = None
        for d in range(4 - t) if fluxes is not None else ():
            term = FIRST[d + t] * fluxes[c, d]
            if c:
                term = term + SECOND[d + t] * smooths[c - 1, d]
            total = term if total is None else total + term
        if total is not None:
            value = value + factor * total
        values.append(value)
    return i, values


def odd_kernel(inner, step, x_rim, y_rim, out, fluxes, smooths, sums):
    x_below, y_below = 1 - odd("y"), 1 - odd("core")
    y_terms(y_below, y_rim, sums)
    x_terms(x_below, x_rim, fluxes, smooths)
    for t in range(8):
        i, values = rim_layer(t, x_below, y_below, inner, step, fluxes, smooths, sums)
        for c in range(5):
            out[c, i] = values[c]


def y_kernel(inner, step, y_rim, out, sums):
    y_below = odd("core")
    y_terms(y_below, y_rim, sums)
    for t in range(8):
        i, values = rim_layer(t, 1, y_below, inner, step, None, None, sums)
        for c in range(5):
            out[c, i] = values[c]


def even_kernel(inner, step, x_rim, out, peak, fluxes, smooths):
    x_below = odd("y")
    x_terms(x_below, x_rim, fluxes, smooths)
    most = None
    for t in range(8):
        i, values = rim_layer(t, x_below, None, inner, step, fluxes, smooths, None)
        for c in range(5):
            out[c, i] = values[c]
        inverse, velocity, kinetic, pressure = primitive(values)
        speed = jnp.sqrt(2.0 * kinetic) + jnp.sqrt(GAMMA * pressure * inverse)
        most = speed if most is None else jnp.maximum(most, speed)
    most = jnp.maximum(most[:, :128], most[:, 128:])
    spread(most, peak)


def spread(values, out):
    out[...] = jnp.broadcast_to(jnp.max(values, axis=0, keepdims=True), out.shape)


def pass_kernel(peaks, out):
    spread(peaks[...], out)


def most_kernel(peaks, out):
    out[0] = jnp.max(peaks[...])


def in_vmem(*sizes):
    return VMEM(sizes, jnp.float32)


def call(kernel, outs, in_specs, scratch, cost, *arrays, out_space=VMEM):
    estimate = pl.CostEstimate(flops=cost * 300, bytes_accessed=cost, transcendentals=0) if cost else None
    return pl.pallas_call(
        kernel,
        out_shape=outs,
        in_specs=[pl.BlockSpec(memory_space=m) for m in in_specs],
        out_specs=tuple(pl.BlockSpec(memory_space=out_space) for _ in outs),
        scratch_shapes=scratch,
        cost_estimate=estimate,
        compiler_params=pltpu.CompilerParams(vmem_limit_bytes=8 << 20),
    )(*arrays)


def far(x):
    return pltpu.with_memory_space_constraint(x, pltpu.HBM)


def swap(x, axis, offset):
    n = lax.axis_size(axis)
    pairs = [((i + offset) % n, (i + 1 + offset) % n) for i in range(0, n, 2)]
    return lax.ppermute(x, axis, pairs + [(b, a) for a, b in pairs])


def local(start, section, previous_speed):
    x_rim, y_rim = in_vmem(5, 4, 16, 256), in_vmem(5, 4, 8, 256)
    (x_odd,) = call(
        first_kernel, (x_rim,), [pltpu.HBM], [pltpu.SemaphoreType.DMA((5,))], 0, far(start)
    )
    y_odd, x_even, y_even = call(pack_kernel, (y_rim, x_rim, y_rim), [VMEM], [], PACK_COST, start)
    x_odd, y_odd = swap(x_odd, GX, 1), swap(y_odd, GY, 1)
    y_even, x_even = swap(y_even, GY, 0), swap(x_even, GX, 0)
    state = in_vmem(5, 8, 16, 256)
    inner, step = call(
        inner_kernel,
        (state, in_vmem(8, 128)),
        [VMEM, VMEM, pltpu.HBM],
        [
            state,
            state,
            in_vmem(4, 8, 16, 256),
            pltpu.SemaphoreType.DMA((2, 5)),
        ],
        INNER_COST,
        previous_speed.reshape(1, 1),
        start,
        far(section),
    )
    rims, sums = [x_rim, in_vmem(4, 4, 16, 256)], in_vmem(5, 8, 8, 256)
    (inner,) = call(
        odd_kernel, (state,), [VMEM] * 4, rims + [sums], ODD_COST, inner, step, x_odd, y_odd
    )
    (inner,) = call(y_kernel, (state,), [VMEM] * 3, [sums], EVEN_COST, inner, step, y_even)
    new, peak = call(
        even_kernel,
        (state, in_vmem(lax.axis_size(NEAR), 128)),
        [VMEM] * 3,
        rims,
        EVEN_COST,
        inner,
        step,
        x_even,
    )
    peaks = lax.all_to_all(peak, NEAR, 0, 0, tiled=True)
    (peak,) = call(pass_kernel, (in_vmem(lax.axis_size(FAR), 128),), [VMEM], [], 0, peaks)
    peaks = lax.all_to_all(peak, FAR, 0, 0, tiled=True)
    (most,) = call(
        most_kernel, (SMEM((1,), jnp.float32),), [VMEM], [], 0, peaks, out_space=SMEM
    )
    return new, most.reshape(())


def solution(mesh):
    split = Mesh(mesh.devices.reshape(SIZES), AXES)
    spec = P(None, GX, GY, None)
    return jax.shard_map(
        local, mesh=split, in_specs=(spec, spec, P()), out_specs=(spec, P()), check_vma=False
    )
```
